32 devices in a mesh: groups: 2 (over y), tile: 4 (over z), pos: 4 (over x, core).
Axes of the slice: x: 2, y: 2, z: 4, core: 2. Of those that a mesh axis runs over, the one named last changes fastest.
Arguments:
- object_field: float32 [4, 2, 256, 1024], P('groups', None, 'tile'), parts along dimension 0, may hold values from -8 to 8
- probe_modes: float32 [8, 2, 128, 128], P('groups'), parts along dimension 0, may hold values from -6 to 6
- measured: float32 [8, 4, 8, 128, 128], P(('groups', 'tile'), 'pos'), parts along dimension 0, may hold values from 0.2 to 2
- row_offset: int32 [8, 4, 8], P(('groups', 'tile'), 'pos'), parts along dimension 0, may hold values from 0 to 63
- col_offset: int32 [8, 4, 8], P(('groups', 'tile'), 'pos'), parts along dimension 0, may hold values from 0 to 896
- position_count: int32 [8, 4], P(('groups', 'tile'), 'pos'), parts along dimension 0, may hold values from 1 to 8, as said below
Outputs:
- object_update: float32 [4, 2, 256, 1024], P('groups', None, 'tile'), parts along dimension 0
- probe_update: float32 [8, 2, 128, 128], P('groups'), parts along dimension 0
The draws below stay inside these ranges and needn't reach their ends.
There are 2 independent parts, one for each index of `groups`. The reference program is written for one: setup_inputs(seed, part) draws one part's arguments, and reference() takes and returns one part's arrays. A program takes and returns all parts, laid end to end along the dimension named above; each array names one. Nothing has to cross between parts.
Inputs may be any that keep to these rules, and one draw needn't show every extreme that they name: `position_count`: every device has at least one live slot and some device has 8.
All inputs are finite; a program needn't handle non-finite values.
Results may differ from the reference program's by a relative error of at most 0.0001.
Values sent between devices are 32-bit elements; how exact they have to be, the bound alone decides.
A program may use at most 64 MiB of HBM per device.

```python
import math
import jax
import jax.numpy as jnp
from jax import lax

SLICES = 2
MODES = 4
PATCH = 128
STRIP = 64
OW = 1024
CAP = 8
STRIPS = 4
REPLICAS = 4
OH = 256


def scale_profile(key, shape, low_end, high_end):
    return jnp.exp(jax.random.uniform(key, shape, jnp.float32, math.log(low_end), math.log(high_end)))


def draw_object_field(key, part):
    key = jax.random.fold_in(key, 11)
    key_base, key_rows, key_cols = jax.random.split(key, 3)
    base = jnp.clip(0.7 * jax.random.normal(key_base, (SLICES, 2, OH, OW), jnp.float32), -2.8, 2.8)
    row_scale = scale_profile(key_rows, (SLICES, 1, OH, 1), 0.6, 1.6)
    col_scale = scale_profile(key_cols, (SLICES, 1, 1, OW), 0.6, 1.6)
    return base * row_scale * col_scale


def draw_probe_modes(key, part):
    key = jax.random.fold_in(key, 17)
    key_base = jax.random.fold_in(key, 0)
    key_rows = jax.random.fold_in(key, 2)
    key_cols = jax.random.fold_in(key, 3)
    base = jnp.clip(0.35 * jax.random.normal(key_base, (MODES, 2, PATCH, PATCH), jnp.float32), -1.4, 1.4)
    row_scale = scale_profile(key_rows, (MODES, 1, PATCH, 1), 0.56, 1.78)
    col_scale = scale_profile(key_cols, (MODES, 1, 1, PATCH), 0.56, 1.78)
    return base * row_scale * col_scale


def draw_position_count(key, part):
    key = jax.random.fold_in(key, 29)
    key_level, key_pick = jax.random.split(key, 2)
    levels = jax.random.randint(key_level, (STRIPS * REPLICAS,), 0, 8)
    counts = jnp.where(levels < 5, 1, jnp.where(levels < 7, max(CAP // 2, 1), CAP)).astype(jnp.int32)
    picked = jax.random.randint(key_pick, (), 0, STRIPS * REPLICAS)
    counts = counts.at[picked].set(CAP)
    return counts.reshape(STRIPS, REPLICAS).astype(jnp.int32)


def set_ends(drawn, own_key, smallest, top_value):
    dims = drawn.shape
    place = [jax.random.randint(jax.random.fold_in(own_key, axis), (), 0, dims[axis]) for axis in range(len(dims))]
    drawn = drawn.at[tuple(place)].set(smallest)
    longest = dims.index(max(dims))
    place[longest] = (place[longest] + 1) % dims[longest]
    return drawn.at[tuple(place)].set(top_value)


def level_of(key, shape, pieces, least, top_value):
    loudness = 1.0
    for axis_at, shards_of in pieces:
        draws = jax.random.uniform(jax.random.fold_in(jax.random.fold_in(key, 6), axis_at), (shards_of,), jnp.float32, least / len(pieces), top_value / len(pieces))
        loudness = loudness * jnp.repeat(jnp.exp(draws), shape[axis_at] // shards_of).reshape((-1,) + (1,) * (len(shape) - 1 - axis_at))
    return loudness


def setup_inputs(seed: int = 0, part: int = 0) -> dict:
    seeds = jax.random.split(jax.random.key(seed), 7)
    own_keys = jax.random.split(jax.random.fold_in(seeds[6], part), 7)
    return {
        "object_field": draw_object_field(jax.random.fold_in(jax.random.fold_in(seeds[6], part), 71), part),
        "probe_modes": draw_probe_modes(jax.random.fold_in(jax.random.fold_in(seeds[6], part), 71), part),
        "measured": jnp.clip(0.2 + 1.8 * jax.random.uniform(own_keys[2], (STRIPS, REPLICAS, CAP, PATCH, PATCH), jnp.float32) ** level_of(own_keys[2], (STRIPS, REPLICAS, CAP, PATCH, PATCH), ((0, 4), (1, 4)), -0.2, 0.2), 0.2, 2.0),
        "row_offset": set_ends(jax.random.randint(own_keys[3], (STRIPS, REPLICAS, CAP), 0, STRIP), jax.random.fold_in(own_keys[3], 1), 0, STRIP - 1).astype(jnp.int32),
        "col_offset": set_ends(jax.random.randint(own_keys[4], (STRIPS, REPLICAS, CAP), 0, OW - PATCH + 1), jax.random.fold_in(own_keys[4], 1), 0, OW - PATCH).astype(jnp.int32),
        "position_count": draw_position_count(jax.random.fold_in(jax.random.fold_in(seeds[6], part), 71), part),
    }


FRESNEL = 0.25
RELAX = 1.0
PROBE_RATE = 4.0

def product_high(left_mat, right_mat):
    return jnp.dot(left_mat, right_mat, precision=lax.Precision.HIGHEST, preferred_element_type=jnp.float32)

def complex_tables():
    indices = jnp.arange(PATCH, dtype=jnp.int32)
    products = indices[:, None] * indices[None, :] % PATCH
    angle_tab = 2.0 * math.pi / PATCH * products.astype(jnp.float32)
    scale_tab = 1.0 / math.sqrt(PATCH)
    fourier_re = jnp.cos(angle_tab) * scale_tab
    fourier_im = -jnp.sin(angle_tab) * scale_tab
    frequency = jnp.where(indices < PATCH // 2, indices, indices - PATCH).astype(jnp.float32) / PATCH
    phase_tab = -math.pi * FRESNEL * PATCH * frequency * frequency
    kernel_re = jnp.cos(phase_tab)
    kernel_im = jnp.sin(phase_tab)
    left_re = fourier_re * kernel_re[None, :] + fourier_im * kernel_im[None, :]
    left_im = fourier_re * kernel_im[None, :] - fourier_im * kernel_re[None, :]
    propagator_re = product_high(left_re, fourier_re) - product_high(left_im, fourier_im)
    propagator_im = product_high(left_re, fourier_im) + product_high(left_im, fourier_re)
    return (fourier_re, fourier_im, propagator_re, propagator_im)

def apply_both(mat_re, mat_im, field_re, field_im):
    highest = lax.Precision.HIGHEST
    half_re = jnp.einsum('ij,mjk->mik', mat_re, field_re, precision=highest) - jnp.einsum('ij,mjk->mik', mat_im, field_im, precision=highest)
    half_im = jnp.einsum('ij,mjk->mik', mat_re, field_im, precision=highest) + jnp.einsum('ij,mjk->mik', mat_im, field_re, precision=highest)
    done_re = jnp.einsum('mij,kj->mik', half_re, mat_re, precision=highest) - jnp.einsum('mij,kj->mik', half_im, mat_im, precision=highest)
    done_im = jnp.einsum('mij,kj->mik', half_re, mat_im, precision=highest) + jnp.einsum('mij,kj->mik', half_im, mat_re, precision=highest)
    return (done_re, done_im)

def slot_loss(patches, probe_modes, measured_one, tables):
    fourier_re, fourier_im, propagator_re, propagator_im = tables
    wave_re = probe_modes[:, 0] * patches[0, 0] - probe_modes[:, 1] * patches[0, 1]
    wave_im = probe_modes[:, 0] * patches[0, 1] + probe_modes[:, 1] * patches[0, 0]
    for layer_id in range(1, SLICES):
        wave_re, wave_im = apply_both(propagator_re, propagator_im, wave_re, wave_im)
        next_re = wave_re * patches[layer_id, 0] - wave_im * patches[layer_id, 1]
        wave_im = wave_re * patches[layer_id, 1] + wave_im * patches[layer_id, 0]
        wave_re = next_re
    detector_re, detector_im = apply_both(fourier_re, fourier_im, wave_re, wave_im)
    intensity = lax.optimization_barrier(jnp.sum(detector_re * detector_re + detector_im * detector_im, axis=0))
    misfit = intensity - measured_one
    return 0.5 * jnp.sum(misfit * misfit)

def reference(object_field, probe_modes, measured, row_offset, col_offset, position_count):
    tables = complex_tables()
    gradient = jax.grad(slot_loss, argnums=(0, 1))
    padded = jnp.concatenate([object_field, jnp.zeros((SLICES, 2, PATCH, OW), jnp.float32)], axis=2)
    top_rows = (jnp.arange(STRIPS, dtype=jnp.int32)[:, None, None] * STRIP + row_offset).reshape(-1).astype(jnp.int32)
    left_cols = col_offset.reshape(-1).astype(jnp.int32)
    live_mask = (jnp.arange(CAP, dtype=jnp.int32)[None, None, :] < position_count[:, :, None]).astype(jnp.float32).reshape(-1)
    measured_all = measured.reshape(-1, PATCH, PATCH)
    lighting = lax.optimization_barrier(jnp.sum(probe_modes[:, 0] * probe_modes[:, 0] + probe_modes[:, 1] * probe_modes[:, 1], axis=0))
    initial = (jnp.zeros((2 * SLICES + 1, OH + PATCH, OW), jnp.float32), jnp.zeros_like(probe_modes), jnp.zeros((PATCH, PATCH), jnp.float32))

    def visit_slot(running, slot_item):
        top_row, left_col, weight, measured_one = slot_item
        stacked, probe_sum, norm_sum = running
        zero_index = jnp.zeros((), jnp.int32)
        patches = lax.dynamic_slice(padded, (zero_index, zero_index, top_row, left_col), (SLICES, 2, PATCH, PATCH))
        patch_grad, probe_grad = gradient(patches, probe_modes, measured_one, tables)
        term = jnp.concatenate([patch_grad.reshape(2 * SLICES, PATCH, PATCH), lighting[None]], axis=0)
        current = lax.dynamic_slice(stacked, (zero_index, top_row, left_col), (2 * SLICES + 1, PATCH, PATCH))
        stacked = lax.dynamic_update_slice(stacked, current + weight * term, (zero_index, top_row, left_col))
        probe_sum = probe_sum + weight * probe_grad
        norm_sum = norm_sum + weight * (patches[0, 0] * patches[0, 0] + patches[0, 1] * patches[0, 1])
        return ((stacked, probe_sum, norm_sum), None)
    outcome = lax.scan(visit_slot, initial, (top_rows, left_cols, live_mask, measured_all))
    stacked, probe_sum, norm_sum = outcome[0]
    summed = stacked[:, :OH]
    object_update = (-summed[:2 * SLICES] / (summed[2 * SLICES][None] + RELAX)).reshape(SLICES, 2, OH, OW)
    probe_update = -PROBE_RATE * probe_sum / (norm_sum[None, None] + RELAX)
    return (object_update, probe_update)
```

```python
import functools
import math

import jax
import jax.numpy as jnp
import numpy as np
from jax import lax
from jax.experimental import pallas as pl
from jax.experimental.pallas import tpu as pltpu
from jax.sharding import PartitionSpec as P

FRESNEL = 0.25
RELAX = 1.0
PROBE_RATE = 4.0
MIB = 1024 * 1024


def passed_along(value, axis, by):
    devices = lax.axis_size(axis)
    pairs = [(i, i + by) for i in range(devices) if 0 <= i + by < devices]
    return lax.ppermute(value, axis, pairs)


def block_tables(side):
    indices = np.arange(side)
    angle = 2.0 * np.pi / side * (indices[:, None] * indices[None, :] % side)
    fourier = np.exp(-1j * angle) / np.sqrt(side)
    frequency = np.where(indices < side // 2, indices, indices - side) / side
    kernel = np.exp(-1j * math.pi * FRESNEL * side * frequency * frequency)
    propagator = (np.conj(fourier) * kernel[None, :]) @ fourier
    blocks = []
    for table in (propagator, np.conj(propagator), fourier, np.conj(fourier)):
        blocks.append(np.block([[table.real, table.imag], [-table.imag, table.real]]))
    stacked = np.stack(blocks).astype(np.float32)
    high = stacked.astype(jnp.bfloat16)
    low = (stacked - high.astype(np.float32)).astype(jnp.bfloat16)
    return high, low


def halves(value):
    high = value.astype(jnp.bfloat16)
    low = (value - high.astype(jnp.float32)).astype(jnp.bfloat16)
    return high, low


def dot(left, right):
    return jnp.dot(left, right, preferred_element_type=jnp.float32)


def both_sides(fields, right_high, right_low, left_high, left_low):
    side = fields[0][0].shape[0]
    rows = jnp.concatenate([jnp.concatenate(field, axis=1) for field in fields], axis=0)
    high, low = halves(rows)
    half = dot(high, right_high) + dot(high, right_low) + dot(low, right_high)
    tops = [half[i * side : (i + 1) * side, :side] for i in range(len(fields))]
    ends = [half[i * side : (i + 1) * side, side:] for i in range(len(fields))]
    cols = jnp.concatenate([jnp.concatenate(tops, axis=1), jnp.concatenate(ends, axis=1)], axis=0)
    high, low = halves(cols)
    done = dot(left_high, high) + dot(left_low, high) + dot(left_high, low)
    return [
        (done[:side, i * side : (i + 1) * side], done[side:, i * side : (i + 1) * side])
        for i in range(len(fields))
    ]


def times(left, right):
    return (left[0] * right[0] - left[1] * right[1], left[0] * right[1] + left[1] * right[0])


def times_conj(left, right):
    return (left[0] * right[0] + left[1] * right[1], left[1] * right[0] - left[0] * right[1])


def slots_kernel(
    row_ref, col_ref, count_ref, object_ref, probe_ref, measured_ref, high_ref, low_ref,
    stacked_ref, probe_sum_ref, norm_ref, light_ref, mid_ref, far_ref,
):
    modes, _, side, _ = probe_ref.shape
    width = object_ref.shape[2]
    stacked_ref[...] = jnp.zeros_like(stacked_ref)
    probe_sum_ref[...] = jnp.zeros_like(probe_sum_ref)
    norm_ref[...] = jnp.zeros_like(norm_ref)
    light = jnp.zeros((side, side), jnp.float32)
    for m in range(modes):
        light = light + probe_ref[m, 0] * probe_ref[m, 0] + probe_ref[m, 1] * probe_ref[m, 1]
    light_ref[...] = light
    groups = [list(range(m, min(m + 2, modes))) for m in range(0, modes, 2)]
    prop, prop_c, four, four_c = range(4)

    def apply(fields, table, conj_table):
        return both_sides(
            fields, high_ref[table], low_ref[table], high_ref[conj_table], low_ref[conj_table]
        )

    def visit(slot, carry):
        row = row_ref[slot]
        col = col_ref[slot]
        base = pl.multiple_of(jnp.minimum(col // 128 * 128, width - 2 * 128), 128)
        offset = col - base
        lane = lax.broadcasted_iota(jnp.int32, (side + 8, 128), 1)
        back = lax.rem(128 - lax.rem(offset, 128), 128)
        ahead = lax.rem(offset, 128)

        start = pl.multiple_of(row // 8 * 8, 8)
        shift = row - start
        tall = side + 8
        rise = lax.rem(tall - shift, tall)

        def patch(plane):
            first = object_ref[plane, pl.ds(start, tall), pl.ds(base, 128)]
            second = object_ref[plane, pl.ds(start, tall), pl.ds(base + 128, 128)]
            chosen = pltpu.roll(jnp.where(lane >= offset, first, second), back, 1)
            return pltpu.roll(chosen, rise, 0)[:side]

        def place(plane, value):
            value = jnp.concatenate([value, jnp.zeros((8, side), jnp.float32)], axis=0)
            value = pltpu.roll(pltpu.roll(value, ahead, 1), shift, 0)
            kept = lane >= offset
            first = jnp.where(kept, value, 0.0)
            second = jnp.where(kept, 0.0, value)
            at = (plane, pl.ds(start, tall), pl.ds(base, 128))
            stacked_ref[at] = stacked_ref[at] + first
            at = (plane, pl.ds(start, tall), pl.ds(base + 128, 128))
            stacked_ref[at] = stacked_ref[at] + second

        upper = (patch(0), patch(1))
        lower = (patch(2), patch(3))
        norm_ref[...] += upper[0] * upper[0] + upper[1] * upper[1]
        place(4, light_ref[...])
        intensity = jnp.zeros((side, side), jnp.float32)
        for group in groups:
            waves = [times((probe_ref[m, 0], probe_ref[m, 1]), upper) for m in group]
            waves = apply(waves, prop, prop_c)
            for m, wave in zip(group, waves):
                mid_ref[m, 0] = wave[0]
                mid_ref[m, 1] = wave[1]
            waves = apply([times(wave, lower) for wave in waves], four, four_c)
            for m, wave in zip(group, waves):
                far_ref[m, 0] = wave[0]
                far_ref[m, 1] = wave[1]
                intensity = intensity + wave[0] * wave[0] + wave[1] * wave[1]
        misfit = 2.0 * (intensity - measured_ref[slot])
        zero = jnp.zeros((side, side), jnp.float32)
        lower_grad = (zero, zero)
        upper_grad = (zero, zero)
        for group in groups:
            grads = [(misfit * far_ref[m, 0], misfit * far_ref[m, 1]) for m in group]
            grads = apply(grads, four_c, four)
            for m, grad in zip(group, grads):
                term = times_conj(grad, (mid_ref[m, 0], mid_ref[m, 1]))
                lower_grad = (lower_grad[0] + term[0], lower_grad[1] + term[1])
            grads = apply([times_conj(grad, lower) for grad in grads], prop_c, prop)
            for m, grad in zip(group, grads):
                term = times_conj(grad, (probe_ref[m, 0], probe_ref[m, 1]))
                upper_grad = (upper_grad[0] + term[0], upper_grad[1] + term[1])
                term = times_conj(grad, upper)
                probe_sum_ref[m, 0] += term[0]
                probe_sum_ref[m, 1] += term[1]
        place(0, upper_grad[0])
        place(1, upper_grad[1])
        place(2, lower_grad[0])
        place(3, lower_grad[1])
        return carry

    lax.fori_loop(0, count_ref[0], visit, 0)


def slots(rows, cols, count, extended, probe_modes, measured):
    modes, _, side, _ = probe_modes.shape
    high, low = block_tables(side)
    planes, ext_rows, width = extended.shape
    vmem = pl.BlockSpec(memory_space=pltpu.VMEM)
    smem = pl.BlockSpec(memory_space=pltpu.SMEM)
    return pl.pallas_call(
        slots_kernel,
        out_shape=(
            jax.ShapeDtypeStruct((planes + 1, ext_rows, width), jnp.float32),
            jax.ShapeDtypeStruct(probe_modes.shape, jnp.float32),
            jax.ShapeDtypeStruct((side, side), jnp.float32),
        ),
        in_specs=[smem] * 3 + [vmem] * 5,
        out_specs=(vmem,) * 3,
        scratch_shapes=[
            pltpu.VMEM((side, side), jnp.float32),
            pltpu.VMEM(probe_modes.shape, jnp.float32),
            pltpu.VMEM(probe_modes.shape, jnp.float32),
        ],
        compiler_params=pltpu.CompilerParams(vmem_limit_bytes=40 * MIB),
        name="slots",
    )(rows, cols, count, extended, probe_modes, measured, jnp.asarray(high), jnp.asarray(low))


def per_device(object_field, probe_modes, measured, row_offset, col_offset, position_count):
    layers, _, strip_rows, width = object_field.shape
    side = probe_modes.shape[2]
    reach = side // strip_rows
    own = object_field.reshape(2 * layers, strip_rows, width)
    below = [passed_along(own, "tile", -by) for by in range(1, reach + 1)]
    extended = jnp.concatenate([own] + below, axis=1)
    stacked, probe_sum, norm_sum = slots(
        row_offset.reshape(-1),
        col_offset.reshape(-1),
        position_count.reshape(-1),
        extended,
        probe_modes,
        measured.reshape(-1, side, side),
    )
    upper_rows = stacked[:, :strip_rows]
    for by in range(1, reach + 1):
        rim_rows = stacked[:, by * strip_rows : (by + 1) * strip_rows]
        upper_rows = upper_rows + passed_along(rim_rows, "tile", by)
    summed = lax.psum(upper_rows, "pos")
    update_flat = -summed[: 2 * layers] / (summed[2 * layers][None] + RELAX)
    object_update = update_flat.reshape(layers, 2, strip_rows, width)
    probe_total, norm_total = lax.psum((probe_sum, norm_sum), ("tile", "pos"))
    probe_update = -PROBE_RATE * probe_total / (norm_total[None, None] + RELAX)
    return (object_update, probe_update)


def solution(mesh):
    return jax.shard_map(
        per_device,
        mesh=mesh,
        in_specs=(
            P("groups", None, "tile", None),
            P("groups", None, None, None),
            P(("groups", "tile"), "pos", None, None, None),
            P(("groups", "tile"), "pos", None),
            P(("groups", "tile"), "pos", None),
            P(("groups", "tile"), "pos"),
        ),
        out_specs=(P("groups", None, "tile", None), P("groups", None, None, None)),
        check_vma=False,
    )
```

```python
import functools
import math

import jax
import jax.numpy as jnp
import numpy as np
from jax import lax
from jax.experimental import pallas as pl
from jax.experimental.pallas import tpu as pltpu
from jax.sharding import PartitionSpec as P

FRESNEL = 0.25
RELAX = 1.0
PROBE_RATE = 4.0
MIB = 1024 * 1024


def block_tables(side):
    indices = np.arange(side)
    angle = 2.0 * np.pi / side * (indices[:, None] * indices[None, :] % side)
    fourier = np.exp(-1j * angle) / np.sqrt(side)
    frequency = np.where(indices < side // 2, indices, indices - side) / side
    kernel = np.exp(-1j * math.pi * FRESNEL * side * frequency * frequency)
    propagator = (np.conj(fourier) * kernel[None, :]) @ fourier
    blocks = []
    for table in (propagator, np.conj(propagator), fourier, np.conj(fourier)):
        blocks.append(np.block([[table.real, table.imag], [-table.imag, table.real]]))
    stacked = np.stack(blocks).astype(np.float32)
    high = stacked.astype(jnp.bfloat16)
    low = (stacked - high.astype(np.float32)).astype(jnp.bfloat16)
    return high, low


def halves(value):
    high = value.astype(jnp.bfloat16)
    low = (value - high.astype(jnp.float32)).astype(jnp.bfloat16)
    return high, low


def dot(left, right):
    return jnp.dot(left, right, preferred_element_type=jnp.float32)


def both_sides(fields, right_high, right_low, left_high, left_low):
    side = fields[0][0].shape[0]
    rows = jnp.concatenate([jnp.concatenate(field, axis=1) for field in fields], axis=0)
    high, low = halves(rows)
    half = dot(high, right_high) + dot(high, right_low) + dot(low, right_high)
    tops = [half[i * side : (i + 1) * side, :side] for i in range(len(fields))]
    ends = [half[i * side : (i + 1) * side, side:] for i in range(len(fields))]
    cols = jnp.concatenate([jnp.concatenate(tops, axis=1), jnp.concatenate(ends, axis=1)], axis=0)
    high, low = halves(cols)
    done = dot(left_high, high) + dot(left_low, high) + dot(left_high, low)
    return [
        (done[:side, i * side : (i + 1) * side], done[side:, i * side : (i + 1) * side])
        for i in range(len(fields))
    ]


def times(left, right):
    return (left[0] * right[0] - left[1] * right[1], left[0] * right[1] + left[1] * right[0])


def times_conj(left, right):
    return (left[0] * right[0] + left[1] * right[1], left[1] * right[0] - left[0] * right[1])


def slots_kernel(
    row_ref, col_ref, count_ref, object_ref, probe_ref, measured_ref, high_ref, low_ref,
    stacked_ref, sums_ref, light_ref, mid_ref, far_ref,
):
    modes, _, side, _ = probe_ref.shape
    width = object_ref.shape[2]
    stacked_ref[...] = jnp.zeros_like(stacked_ref)
    sums_ref[...] = jnp.zeros_like(sums_ref)
    light = jnp.zeros((side, side), jnp.float32)
    for m in range(modes):
        light = light + probe_ref[m, 0] * probe_ref[m, 0] + probe_ref[m, 1] * probe_ref[m, 1]
    light_ref[...] = light
    groups = [list(range(m, min(m + 2, modes))) for m in range(0, modes, 2)]
    prop, prop_c, four, four_c = range(4)

    def apply(fields, table, conj_table):
        return both_sides(
            fields, high_ref[table], low_ref[table], high_ref[conj_table], low_ref[conj_table]
        )

    def visit(slot, carry):
        row = row_ref[slot]
        col = col_ref[slot]
        base = pl.multiple_of(jnp.minimum(col // 128 * 128, width - 2 * 128), 128)
        offset = col - base
        lane = lax.broadcasted_iota(jnp.int32, (side + 8, 128), 1)
        back = lax.rem(128 - lax.rem(offset, 128), 128)
        ahead = lax.rem(offset, 128)

        start = pl.multiple_of(row // 8 * 8, 8)
        shift = row - start
        tall = side + 8
        rise = lax.rem(tall - shift, tall)

        def patch(plane):
            first = object_ref[plane, pl.ds(start, tall), pl.ds(base, 128)]
            second = object_ref[plane, pl.ds(start, tall), pl.ds(base + 128, 128)]
            chosen = pltpu.roll(jnp.where(lane >= offset, first, second), back, 1)
            return pltpu.roll(chosen, rise, 0)[:side]

        def place(plane, value):
            value = jnp.concatenate([value, jnp.zeros((8, side), jnp.float32)], axis=0)
            value = pltpu.roll(pltpu.roll(value, ahead, 1), shift, 0)
            kept = lane >= offset
            first = jnp.where(kept, value, 0.0)
            second = jnp.where(kept, 0.0, value)
            at = (plane, pl.ds(start, tall), pl.ds(base, 128))
            stacked_ref[at] = stacked_ref[at] + first
            at = (plane, pl.ds(start, tall), pl.ds(base + 128, 128))
            stacked_ref[at] = stacked_ref[at] + second

        upper = (patch(0), patch(1))
        lower = (patch(2), patch(3))
        sums_ref[2 * modes] += upper[0] * upper[0] + upper[1] * upper[1]
        place(4, light_ref[...])
        intensity = jnp.zeros((side, side), jnp.float32)
        for group in groups:
            waves = [times((probe_ref[m, 0], probe_ref[m, 1]), upper) for m in group]
            waves = apply(waves, prop, prop_c)
            for m, wave in zip(group, waves):
                mid_ref[m, 0] = wave[0]
                mid_ref[m, 1] = wave[1]
            waves = apply([times(wave, lower) for wave in waves], four, four_c)
            for m, wave in zip(group, waves):
                far_ref[m, 0] = wave[0]
                far_ref[m, 1] = wave[1]
                intensity = intensity + wave[0] * wave[0] + wave[1] * wave[1]
        misfit = 2.0 * (intensity - measured_ref[slot])
        zero = jnp.zeros((side, side), jnp.float32)
        lower_grad = (zero, zero)
        upper_grad = (zero, zero)
        for group in groups:
            grads = [(misfit * far_ref[m, 0], misfit * far_ref[m, 1]) for m in group]
            grads = apply(grads, four_c, four)
            for m, grad in zip(group, grads):
                term = times_conj(grad, (mid_ref[m, 0], mid_ref[m, 1]))
                lower_grad = (lower_grad[0] + term[0], lower_grad[1] + term[1])
            grads = apply([times_conj(grad, lower) for grad in grads], prop_c, prop)
            for m, grad in zip(group, grads):
                term = times_conj(grad, (probe_ref[m, 0], probe_ref[m, 1]))
                upper_grad = (upper_grad[0] + term[0], upper_grad[1] + term[1])
                term = times_conj(grad, upper)
                sums_ref[2 * m] += term[0]
                sums_ref[2 * m + 1] += term[1]
        place(0, upper_grad[0])
        place(1, upper_grad[1])
        place(2, lower_grad[0])
        place(3, lower_grad[1])
        return carry

    lax.fori_loop(0, count_ref[0], visit, 0)


def slots(rows, cols, count, extended, probe_modes, measured):
    modes, _, side, _ = probe_modes.shape
    high, low = block_tables(side)
    planes, ext_rows, width = extended.shape
    vmem = pl.BlockSpec(memory_space=pltpu.VMEM)
    smem = pl.BlockSpec(memory_space=pltpu.SMEM)
    return pl.pallas_call(
        slots_kernel,
        out_shape=(
            jax.ShapeDtypeStruct((planes + 1, ext_rows, width), jnp.float32),
            jax.ShapeDtypeStruct((2 * modes + 1, side, side), jnp.float32),
        ),
        in_specs=[smem] * 3 + [vmem] * 5,
        out_specs=(vmem,) * 2,
        scratch_shapes=[
            pltpu.VMEM((side, side), jnp.float32),
            pltpu.VMEM(probe_modes.shape, jnp.float32),
            pltpu.VMEM(probe_modes.shape, jnp.float32),
        ],
        compiler_params=pltpu.CompilerParams(vmem_limit_bytes=40 * MIB),
        name="slots",
    )(rows, cols, count, extended, probe_modes, measured, jnp.asarray(high), jnp.asarray(low))


def flipped(index, bit):
    return index + bit - 2 * bit * (index // bit % 2)


def greet(peers):
    barrier = pltpu.get_barrier_semaphore()
    for peer in peers:
        pl.semaphore_signal(barrier, inc=1, device_id=peer, device_id_type=pl.DeviceIdType.MESH)
    pl.semaphore_wait(barrier, len(peers))


def remote(source, target, send_sem, recv_sem, peer):
    return pltpu.make_async_remote_copy(
        src_ref=source,
        dst_ref=target,
        send_sem=send_sem,
        recv_sem=recv_sem,
        device_id=peer,
        device_id_type=pl.DeviceIdType.MESH,
    )


class Places:
    def __init__(self):
        self.tiles = lax.axis_size("tile")
        self.replicas = lax.axis_size("pos")
        self.tile = lax.axis_index("tile")
        self.own = lax.axis_index("pos")
        self.near = flipped(self.own, 1)
        self.far = flipped(self.own, 2)
        self.cross = flipped(self.near, 2)
        self.near_id = {"pos": self.near}
        self.far_id = {"pos": self.far}
        self.up_id = {"tile": lax.rem(self.tile + self.tiles - 1, self.tiles)}
        self.down_id = {"tile": lax.rem(self.tile + 1, self.tiles)}

    def rows(self, first, quarter, count):
        return pl.ds(pl.multiple_of(first + quarter * count, 8), count)


def halo_kernel(own_ref, ext_ref, tile_send, tile_recv, far_send, far_recv, near_send, near_recv):
    at = Places()
    strip = own_ref.shape[1]
    part = strip // at.replicas
    reach = ext_ref.shape[1] // strip - 1
    greet([at.near_id, at.far_id, at.up_id, at.down_id])

    def slot(k, quarter):
        return ext_ref.at[:, at.rows(k * strip, quarter, part)]

    def up(k):
        if k == 1:
            source = own_ref.at[:, at.rows(0, at.own, part)]
        else:
            source = slot(k - 1, at.own)
        return remote(source, slot(k, at.own), tile_send.at[k - 1], tile_recv.at[k - 1], at.up_id)

    def across(k, quarter):
        return remote(slot(k, quarter), slot(k, quarter), far_send.at[k - 1], far_recv.at[k - 1], at.far_id)

    def beside(k, which, quarter):
        return remote(
            slot(k, quarter), slot(k, quarter), near_send.at[k - 1, which], near_recv.at[k - 1, which], at.near_id
        )

    def sends(k):
        return jnp.logical_and(at.tile > 0, at.tile + k - 1 < at.tiles)

    @pl.when(sends(1))
    def _():
        up(1).start()

    ext_ref[:, :strip] = own_ref[...]
    for k in range(1, reach + 1):
        @pl.when(at.tile + k >= at.tiles)
        def _(k=k):
            ext_ref[:, k * strip : (k + 1) * strip] = jnp.zeros(own_ref.shape, jnp.float32)

    for k in range(1, reach + 1):
        @pl.when(at.tile + k < at.tiles)
        def _(k=k):
            up(k).wait_recv()

        if k < reach:
            @pl.when(sends(k + 1))
            def _(k=k):
                up(k + 1).start()

        @pl.when(at.tile + k < at.tiles)
        def _(k=k):
            across(k, at.own).start()
            beside(k, 0, at.own).start()

        if k > 1:
            @pl.when(at.tile + k - 1 < at.tiles)
            def _(k=k):
                across(k - 1, at.far).wait_recv()
                beside(k - 1, 1, at.far).start()

    @pl.when(at.tile + reach < at.tiles)
    def _():
        across(reach, at.far).wait_recv()
        beside(reach, 1, at.far).start()

    for k in range(1, reach + 1):
        @pl.when(sends(k))
        def _(k=k):
            up(k).wait_send()

        @pl.when(at.tile + k < at.tiles)
        def _(k=k):
            beside(k, 0, at.near).wait_recv()
            beside(k, 1, at.cross).wait_recv()
            across(k, at.own).wait_send()
            beside(k, 0, at.own).wait_send()
            beside(k, 1, at.far).wait_send()


def halo(own, reach, replicas):
    planes, strip, width = own.shape
    vmem = pl.BlockSpec(memory_space=pltpu.VMEM)
    dma = pltpu.SemaphoreType.DMA
    return pl.pallas_call(
        halo_kernel,
        out_shape=jax.ShapeDtypeStruct((planes, strip * (reach + 1), width), jnp.float32),
        in_specs=[vmem],
        out_specs=vmem,
        scratch_shapes=[
            dma((reach,)), dma((reach,)), dma((reach,)), dma((reach,)), dma((reach, 2)), dma((reach, 2))
        ],
        compiler_params=pltpu.CompilerParams(
            collective_id=0, has_side_effects=True, vmem_limit_bytes=40 * MIB
        ),
        name="halo",
    )(own)


def reduce_kernel(
    stacked_ref, sums_ref, object_ref, probe_ref,
    near_land, far_out, far_land, kept, rim_land, sum_near, sum_far, sum_land, sum_steps, step_land,
    near_send, near_recv, far_send, far_recv, rim_send, rim_recv,
    pn_send, pn_recv, pf_send, pf_recv, step_send, step_recv, out_send, out_recv,
):
    at = Places()
    strip = object_ref.shape[1]
    part = strip // at.replicas
    planes = object_ref.shape[0]
    strips = stacked_ref.shape[1] // strip
    sum_part = sums_ref.shape[1] // at.replicas
    steps = at.tiles.bit_length() - 1
    partners = [{"tile": flipped(at.tile, 2**i)} for i in range(steps)]
    greet([at.near_id, at.far_id, at.up_id, at.down_id] + partners)

    def rows(k, quarter):
        return at.rows(k * strip, quarter, part)

    def sum_rows(quarter):
        return at.rows(0, quarter, sum_part)

    def sum_beside(which, quarter):
        return remote(
            sums_ref.at[:, sum_rows(quarter)], sum_near.at[which], pn_send.at[which], pn_recv.at[which], at.near_id
        )

    def beside(k, which, quarter):
        return remote(
            stacked_ref.at[:, rows(k, quarter)], near_land.at[k, which],
            near_send.at[k, which], near_recv.at[k, which], at.near_id,
        )

    def across(k):
        return remote(far_out.at[k], far_land.at[k], far_send.at[k], far_recv.at[k], at.far_id)

    def down(k):
        return remote(kept.at[k], rim_land.at[k - 1], rim_send.at[k - 1], rim_recv.at[k - 1], at.down_id)

    def step(i):
        return remote(sum_steps.at[i], step_land.at[i], step_send.at[i], step_recv.at[i], partners[i])

    sum_across = remote(sum_far, sum_land, pf_send, pf_recv, at.far_id)

    sum_beside(1, at.cross).start()
    sum_beside(0, at.near).start()
    order = list(range(strips - 1, -1, -1))
    for k in order:
        beside(k, 1, at.cross).start()
        beside(k, 0, at.near).start()

    sum_beside(1, at.cross).wait_recv()
    sum_far[...] = sums_ref[:, sum_rows(at.far)] + sum_near[1]
    sum_across.start()
    for k in order:
        beside(k, 1, at.cross).wait_recv()
        far_out[k] = stacked_ref[:, rows(k, at.far)] + near_land[k, 1]
        across(k).start()
    sum_beside(0, at.near).wait_recv()
    total = sums_ref[:, sum_rows(at.own)] + sum_near[0]
    sum_across.wait_recv()
    sum_steps[0] = total + sum_land[...]
    if steps:
        step(0).start()
    for k in order:
        beside(k, 0, at.near).wait_recv()
        across(k).wait_recv()
        kept[k] = stacked_ref[:, rows(k, at.own)] + near_land[k, 0] + far_land[k]
        if k < strips - 1:
            @pl.when(at.tile > 0)
            def _(k=k):
                down(k + 1).wait_recv()
                kept[k] += rim_land[k]

        if k > 0:
            @pl.when(at.tile < at.tiles - 1)
            def _(k=k):
                down(k).start()

        i = strips - 1 - k
        if i < min(steps, strips - 1):
            step(i).wait_recv()
            sum_steps[i + 1] = sum_steps[i] + step_land[i]
            if i + 1 < steps:
                step(i + 1).start()
    for i in range(min(steps, strips - 1), steps):
        step(i).wait_recv()
        sum_steps[i + 1] = sum_steps[i] + step_land[i]
        if i + 1 < steps:
            step(i + 1).start()

    def out(ref, which, lane, quarter, count, peer):
        place = ref.at[:, at.rows(0, quarter, count)]
        return remote(place, place, out_send.at[which, lane], out_recv.at[which, lane], peer)

    probe_ref[:, sum_rows(at.own)] = (
        -PROBE_RATE * sum_steps[steps, : 2 * (sums_ref.shape[0] // 2)] / (sum_steps[steps, 2 * (sums_ref.shape[0] // 2)] + RELAX)
    )
    outs = [(probe_ref, 0, sum_part), (object_ref, 1, part)]
    ref, which, count = outs[0]
    out(ref, which, 0, at.own, count, at.far_id).start()
    out(ref, which, 1, at.own, count, at.near_id).start()
    object_ref[:, rows(0, at.own)] = -kept[0, :planes] / (kept[0, planes] + RELAX)
    ref, which, count = outs[1]
    out(ref, which, 0, at.own, count, at.far_id).start()
    out(ref, which, 1, at.own, count, at.near_id).start()
    for ref, which, count in outs:
        out(ref, which, 0, at.far, count, at.far_id).wait_recv()
        out(ref, which, 2, at.far, count, at.near_id).start()
    for ref, which, count in outs:
        out(ref, which, 1, at.near, count, at.near_id).wait_recv()
        out(ref, which, 2, at.cross, count, at.near_id).wait_recv()
        out(ref, which, 0, at.own, count, at.far_id).wait_send()
        out(ref, which, 1, at.own, count, at.near_id).wait_send()
        out(ref, which, 2, at.far, count, at.near_id).wait_send()

    sum_beside(1, at.cross).wait_send()
    sum_beside(0, at.near).wait_send()
    sum_across.wait_send()
    for k in order:
        beside(k, 1, at.cross).wait_send()
        beside(k, 0, at.near).wait_send()
        across(k).wait_send()
        if k > 0:
            @pl.when(at.tile < at.tiles - 1)
            def _(k=k):
                down(k).wait_send()
    for i in range(steps):
        step(i).wait_send()


def reduced(stacked, sums, strip, tiles, replicas):
    planes, ext_rows, width = stacked.shape
    strips = ext_rows // strip
    part = strip // replicas
    sum_planes, side, _ = sums.shape
    sum_part = side // replicas
    steps = tiles.bit_length() - 1
    vmem = pl.BlockSpec(memory_space=pltpu.VMEM)
    dma = pltpu.SemaphoreType.DMA
    block = (planes, part, width)
    sum_block = (sum_planes, sum_part, side)

    def buffer(*shape):
        return pltpu.VMEM(shape, jnp.float32)

    return pl.pallas_call(
        reduce_kernel,
        out_shape=(
            jax.ShapeDtypeStruct((planes - 1, strip, width), jnp.float32),
            jax.ShapeDtypeStruct((sum_planes - 1, side, side), jnp.float32),
        ),
        in_specs=[vmem, vmem],
        out_specs=(vmem, vmem),
        scratch_shapes=[
            buffer(strips, 2, *block),
            buffer(strips, *block),
            buffer(strips, *block),
            buffer(strips, *block),
            buffer(strips - 1, *block),
            buffer(2, *sum_block),
            buffer(*sum_block),
            buffer(*sum_block),
            buffer(steps + 1, *sum_block),
            buffer(max(steps, 1), *sum_block),
            dma((strips, 2)), dma((strips, 2)), dma((strips,)), dma((strips,)), dma((strips - 1,)), dma((strips - 1,)),
            dma((2,)), dma((2,)), dma, dma, dma((max(steps, 1),)), dma((max(steps, 1),)), dma((2, 3)), dma((2, 3)),
        ],
        compiler_params=pltpu.CompilerParams(
            collective_id=1, has_side_effects=True, vmem_limit_bytes=48 * MIB
        ),
        name="reduce",
    )(stacked, sums)


def per_device(object_field, probe_modes, measured, row_offset, col_offset, position_count):
    layers, _, strip_rows, width = object_field.shape
    side = probe_modes.shape[2]
    reach = side // strip_rows
    tiles = lax.axis_size("tile")
    replicas = lax.axis_size("pos")
    own = object_field.reshape(2 * layers, strip_rows, width)
    extended = halo(own, reach, replicas)
    stacked, sums = slots(
        row_offset.reshape(-1),
        col_offset.reshape(-1),
        position_count.reshape(-1),
        extended,
        probe_modes,
        measured.reshape(-1, side, side),
    )
    object_flat, probe_flat = reduced(stacked, sums, strip_rows, tiles, replicas)
    return object_flat.reshape(object_field.shape), probe_flat.reshape(probe_modes.shape)


def solution(mesh):
    return jax.shard_map(
        per_device,
        mesh=mesh,
        in_specs=(
            P("groups", None, "tile", None),
            P("groups", None, None, None),
            P(("groups", "tile"), "pos", None, None, None),
            P(("groups", "tile"), "pos", None),
            P(("groups", "tile"), "pos", None),
            P(("groups", "tile"), "pos"),
        ),
        out_specs=(P("groups", None, "tile", None), P("groups", None, None, None)),
        check_vma=False,
    )
```

```python
import functools
import math

import jax
import jax.numpy as jnp
import numpy as np
from jax import lax
from jax.experimental import pallas as pl
from jax.experimental.pallas import tpu as pltpu
from jax.sharding import PartitionSpec as P

FRESNEL = 0.25
RELAX = 1.0
PROBE_RATE = 4.0
MIB = 1024 * 1024


def block_tables(side):
    indices = np.arange(side)
    angle = 2.0 * np.pi / side * (indices[:, None] * indices[None, :] % side)
    fourier = np.exp(-1j * angle) / np.sqrt(side)
    frequency = np.where(indices < side // 2, indices, indices - side) / side
    kernel = np.exp(-1j * math.pi * FRESNEL * side * frequency * frequency)
    propagator = (np.conj(fourier) * kernel[None, :]) @ fourier
    blocks = []
    for table in (propagator, np.conj(propagator), fourier, np.conj(fourier)):
        blocks.append(np.block([[table.real, table.imag], [-table.imag, table.real]]))
    stacked = np.stack(blocks).astype(np.float32)
    high = stacked.astype(jnp.bfloat16)
    low = (stacked - high.astype(np.float32)).astype(jnp.bfloat16)
    return high, low


def halves(value):
    high = value.astype(jnp.bfloat16)
    low = (value - high.astype(jnp.float32)).astype(jnp.bfloat16)
    return high, low


def dot(left, right):
    return jnp.dot(left, right, preferred_element_type=jnp.float32)


def both_sides(fields, right_high, right_low, left_high, left_low):
    side = fields[0][0].shape[0]
    rows = jnp.concatenate([jnp.concatenate(field, axis=1) for field in fields], axis=0)
    high, low = halves(rows)
    half = dot(high, right_high) + dot(high, right_low) + dot(low, right_high)
    tops = [half[i * side : (i + 1) * side, :side] for i in range(len(fields))]
    ends = [half[i * side : (i + 1) * side, side:] for i in range(len(fields))]
    cols = jnp.concatenate([jnp.concatenate(tops, axis=1), jnp.concatenate(ends, axis=1)], axis=0)
    high, low = halves(cols)
    done = dot(left_high, high) + dot(left_low, high) + dot(left_high, low)
    return [
        (done[:side, i * side : (i + 1) * side], done[side:, i * side : (i + 1) * side])
        for i in range(len(fields))
    ]


def times(left, right):
    return (left[0] * right[0] - left[1] * right[1], left[0] * right[1] + left[1] * right[0])


def times_conj(left, right):
    return (left[0] * right[0] + left[1] * right[1], left[1] * right[0] - left[0] * right[1])


def slots_kernel(
    info_ref, object_ref, probe_ref, measured_ref, high_ref, low_ref,
    stacked_ref, sums_ref, light_ref, mid_ref, far_ref,
):
    modes, _, side, _ = probe_ref.shape
    width = object_ref.shape[2]
    stacked_ref[...] = jnp.zeros_like(stacked_ref)
    sums_ref[...] = jnp.zeros_like(sums_ref)
    light = jnp.zeros((side, side), jnp.float32)
    for m in range(modes):
        light = light + probe_ref[m, 0] * probe_ref[m, 0] + probe_ref[m, 1] * probe_ref[m, 1]
    light_ref[...] = light
    groups = [list(range(m, min(m + 2, modes))) for m in range(0, modes, 2)]
    prop, prop_c, four, four_c = range(4)

    def apply(fields, table, conj_table):
        return both_sides(
            fields, high_ref[table], low_ref[table], high_ref[conj_table], low_ref[conj_table]
        )

    parity = lax.rem(lax.axis_index("pos"), 2)
    count_even = info_ref[0, 2, 0]
    count_all = count_even + info_ref[1, 2, 0]
    half = (count_all + 1) // 2
    first_slot = parity * half
    last_slot = jnp.where(parity == 0, half, count_all)

    def visit(slot, carry):
        second = (slot >= count_even).astype(jnp.int32)
        within = slot - second * count_even
        row = info_ref[second, 0, within]
        col = info_ref[second, 1, within]
        base = pl.multiple_of(jnp.minimum(col // 128 * 128, width - 2 * 128), 128)
        offset = col - base
        lane = lax.broadcasted_iota(jnp.int32, (side + 8, 128), 1)
        back = lax.rem(128 - lax.rem(offset, 128), 128)
        ahead = lax.rem(offset, 128)

        start = pl.multiple_of(row // 8 * 8, 8)
        shift = row - start
        tall = side + 8
        rise = lax.rem(tall - shift, tall)

        def patch(plane):
            left = object_ref[plane, pl.ds(start, tall), pl.ds(base, 128)]
            right = object_ref[plane, pl.ds(start, tall), pl.ds(base + 128, 128)]
            chosen = pltpu.roll(jnp.where(lane >= offset, left, right), back, 1)
            return pltpu.roll(chosen, rise, 0)[:side]

        def place(plane, value):
            value = jnp.concatenate([value, jnp.zeros((8, side), jnp.float32)], axis=0)
            value = pltpu.roll(pltpu.roll(value, ahead, 1), shift, 0)
            kept = lane >= offset
            left = jnp.where(kept, value, 0.0)
            right = jnp.where(kept, 0.0, value)
            at = (plane, pl.ds(start, tall), pl.ds(base, 128))
            stacked_ref[at] = stacked_ref[at] + left
            at = (plane, pl.ds(start, tall), pl.ds(base + 128, 128))
            stacked_ref[at] = stacked_ref[at] + right

        upper = (patch(0), patch(1))
        lower = (patch(2), patch(3))
        sums_ref[2 * modes] += upper[0] * upper[0] + upper[1] * upper[1]
        place(4, light_ref[...])
        intensity = jnp.zeros((side, side), jnp.float32)
        for group in groups:
            waves = [times((probe_ref[m, 0], probe_ref[m, 1]), upper) for m in group]
            waves = apply(waves, prop, prop_c)
            for m, wave in zip(group, waves):
                mid_ref[m, 0] = wave[0]
                mid_ref[m, 1] = wave[1]
            waves = apply([times(wave, lower) for wave in waves], four, four_c)
            for m, wave in zip(group, waves):
                far_ref[m, 0] = wave[0]
                far_ref[m, 1] = wave[1]
                intensity = intensity + wave[0] * wave[0] + wave[1] * wave[1]
        misfit = 2.0 * (intensity - measured_ref[second, within])
        zero = jnp.zeros((side, side), jnp.float32)
        lower_grad = (zero, zero)
        upper_grad = (zero, zero)
        for group in groups:
            grads = [(misfit * far_ref[m, 0], misfit * far_ref[m, 1]) for m in group]
            grads = apply(grads, four_c, four)
            for m, grad in zip(group, grads):
                term = times_conj(grad, (mid_ref[m, 0], mid_ref[m, 1]))
                lower_grad = (lower_grad[0] + term[0], lower_grad[1] + term[1])
            grads = apply([times_conj(grad, lower) for grad in grads], prop_c, prop)
            for m, grad in zip(group, grads):
                term = times_conj(grad, (probe_ref[m, 0], probe_ref[m, 1]))
                upper_grad = (upper_grad[0] + term[0], upper_grad[1] + term[1])
                term = times_conj(grad, upper)
                sums_ref[2 * m] += term[0]
                sums_ref[2 * m + 1] += term[1]
        place(0, upper_grad[0])
        place(1, upper_grad[1])
        place(2, lower_grad[0])
        place(3, lower_grad[1])
        return carry

    lax.fori_loop(first_slot, last_slot, visit, 0)


def slots(info, extended, probe_modes, measured):
    modes, _, side, _ = probe_modes.shape
    high, low = block_tables(side)
    planes, ext_rows, width = extended.shape
    vmem = pl.BlockSpec(memory_space=pltpu.VMEM)
    smem = pl.BlockSpec(memory_space=pltpu.SMEM)
    return pl.pallas_call(
        slots_kernel,
        out_shape=(
            jax.ShapeDtypeStruct((planes + 1, ext_rows, width), jnp.float32),
            jax.ShapeDtypeStruct((2 * modes + 1, side, side), jnp.float32),
        ),
        in_specs=[smem] + [vmem] * 5,
        out_specs=(vmem,) * 2,
        scratch_shapes=[
            pltpu.VMEM((side, side), jnp.float32),
            pltpu.VMEM(probe_modes.shape, jnp.float32),
            pltpu.VMEM(probe_modes.shape, jnp.float32),
        ],
        compiler_params=pltpu.CompilerParams(vmem_limit_bytes=40 * MIB),
        name="slots",
    )(info, extended, probe_modes, measured, jnp.asarray(high), jnp.asarray(low))


def flipped(index, bit):
    return index + bit - 2 * bit * (index // bit % 2)


def greet(peers):
    barrier = pltpu.get_barrier_semaphore()
    for peer in peers:
        pl.semaphore_signal(barrier, inc=1, device_id=peer, device_id_type=pl.DeviceIdType.MESH)
    pl.semaphore_wait(barrier, len(peers))


def remote(source, target, send_sem, recv_sem, peer):
    return pltpu.make_async_remote_copy(
        src_ref=source,
        dst_ref=target,
        send_sem=send_sem,
        recv_sem=recv_sem,
        device_id=peer,
        device_id_type=pl.DeviceIdType.MESH,
    )


class Places:
    def __init__(self):
        self.tiles = lax.axis_size("tile")
        self.replicas = lax.axis_size("pos")
        self.tile = lax.axis_index("tile")
        self.own = lax.axis_index("pos")
        self.near = flipped(self.own, 1)
        self.far = flipped(self.own, 2)
        self.cross = flipped(self.near, 2)
        self.near_id = {"pos": self.near}
        self.far_id = {"pos": self.far}
        self.up_id = {"tile": lax.rem(self.tile + self.tiles - 1, self.tiles)}
        self.down_id = {"tile": lax.rem(self.tile + 1, self.tiles)}

    def rows(self, first, quarter, count):
        return pl.ds(pl.multiple_of(first + quarter * count, 8), count)


def halo_kernel(
    own_ref, info_ref, measured_ref, ext_ref, info_pair, measured_pair,
    tile_send, tile_recv, far_send, far_recv, near_send, near_recv, pair_send, pair_recv,
):
    at = Places()
    strip = own_ref.shape[1]
    part = strip // at.replicas
    reach = ext_ref.shape[1] // strip - 1
    greet([at.near_id, at.far_id, at.up_id, at.down_id])

    def slot(k, quarter):
        return ext_ref.at[:, at.rows(k * strip, quarter, part)]

    def up(k):
        if k == 1:
            source = own_ref.at[:, at.rows(0, at.own, part)]
        else:
            source = slot(k - 1, at.own)
        return remote(source, slot(k, at.own), tile_send.at[k - 1], tile_recv.at[k - 1], at.up_id)

    def across(k, quarter):
        return remote(slot(k, quarter), slot(k, quarter), far_send.at[k - 1], far_recv.at[k - 1], at.far_id)

    def beside(k, which, quarter):
        return remote(
            slot(k, quarter), slot(k, quarter), near_send.at[k - 1, which], near_recv.at[k - 1, which], at.near_id
        )

    def sends(k):
        return jnp.logical_and(at.tile > 0, at.tile + k - 1 < at.tiles)

    @pl.when(sends(1))
    def _():
        up(1).start()

    parity = lax.rem(at.own, 2)

    def share(i, place):
        source = (info_ref, measured_ref)[i]
        pair = (info_pair, measured_pair)[i]
        return remote(source, pair.at[place], pair_send.at[i], pair_recv.at[i], at.near_id)

    share(0, parity).start()
    share(1, parity).start()
    info_pair[parity] = info_ref[...]
    measured_pair[parity] = measured_ref[...]
    ext_ref[:, :strip] = own_ref[...]
    for k in range(1, reach + 1):
        @pl.when(at.tile + k >= at.tiles)
        def _(k=k):
            ext_ref[:, k * strip : (k + 1) * strip] = jnp.zeros(own_ref.shape, jnp.float32)

    for k in range(1, reach + 1):
        @pl.when(at.tile + k < at.tiles)
        def _(k=k):
            up(k).wait_recv()

        if k < reach:
            @pl.when(sends(k + 1))
            def _(k=k):
                up(k + 1).start()

        @pl.when(at.tile + k < at.tiles)
        def _(k=k):
            across(k, at.own).start()
            beside(k, 0, at.own).start()

        if k > 1:
            @pl.when(at.tile + k - 1 < at.tiles)
            def _(k=k):
                across(k - 1, at.far).wait_recv()
                beside(k - 1, 1, at.far).start()

    @pl.when(at.tile + reach < at.tiles)
    def _():
        across(reach, at.far).wait_recv()
        beside(reach, 1, at.far).start()

    for k in range(1, reach + 1):
        @pl.when(sends(k))
        def _(k=k):
            up(k).wait_send()

        @pl.when(at.tile + k < at.tiles)
        def _(k=k):
            beside(k, 0, at.near).wait_recv()
            beside(k, 1, at.cross).wait_recv()
            across(k, at.own).wait_send()
            beside(k, 0, at.own).wait_send()
            beside(k, 1, at.far).wait_send()

    for i in range(2):
        share(i, 1 - parity).wait_recv()
        share(i, parity).wait_send()


def halo(own, info, measured, reach):
    planes, strip, width = own.shape
    vmem = pl.BlockSpec(memory_space=pltpu.VMEM)
    dma = pltpu.SemaphoreType.DMA
    return pl.pallas_call(
        halo_kernel,
        out_shape=(
            jax.ShapeDtypeStruct((planes, strip * (reach + 1), width), jnp.float32),
            jax.ShapeDtypeStruct((2,) + info.shape, jnp.int32),
            jax.ShapeDtypeStruct((2,) + measured.shape, jnp.float32),
        ),
        in_specs=[vmem] * 3,
        out_specs=(vmem,) * 3,
        scratch_shapes=[
            dma((reach,)), dma((reach,)), dma((reach,)), dma((reach,)), dma((reach, 2)), dma((reach, 2)),
            dma((2,)), dma((2,)),
        ],
        compiler_params=pltpu.CompilerParams(
            collective_id=0, has_side_effects=True, vmem_limit_bytes=40 * MIB
        ),
        name="halo",
    )(own, info, measured)


def reduce_kernel(
    stacked_ref, sums_ref, object_ref, probe_ref,
    near_land, far_out, far_land, kept, rim_land, sum_near, sum_far, sum_land, sum_steps, step_land,
    near_send, near_recv, far_send, far_recv, rim_send, rim_recv,
    pn_send, pn_recv, pf_send, pf_recv, step_send, step_recv, out_send, out_recv,
):
    at = Places()
    strip = object_ref.shape[1]
    part = strip // at.replicas
    planes = object_ref.shape[0]
    strips = stacked_ref.shape[1] // strip
    sum_part = sums_ref.shape[1] // at.replicas
    steps = at.tiles.bit_length() - 1
    partners = [{"tile": flipped(at.tile, 2**i)} for i in range(steps)]
    greet([at.near_id, at.far_id, at.up_id, at.down_id] + partners)

    def rows(k, quarter):
        return at.rows(k * strip, quarter, part)

    def sum_rows(quarter):
        return at.rows(0, quarter, sum_part)

    def sum_beside(which, quarter):
        return remote(
            sums_ref.at[:, sum_rows(quarter)], sum_near.at[which], pn_send.at[which], pn_recv.at[which], at.near_id
        )

    def beside(k, which, quarter):
        return remote(
            stacked_ref.at[:, rows(k, quarter)], near_land.at[k, which],
            near_send.at[k, which], near_recv.at[k, which], at.near_id,
        )

    def across(k):
        return remote(far_out.at[k], far_land.at[k], far_send.at[k], far_recv.at[k], at.far_id)

    def down(k):
        return remote(kept.at[k], rim_land.at[k - 1], rim_send.at[k - 1], rim_recv.at[k - 1], at.down_id)

    def step(i):
        return remote(sum_steps.at[i], step_land.at[i], step_send.at[i], step_recv.at[i], partners[i])

    sum_across = remote(sum_far, sum_land, pf_send, pf_recv, at.far_id)

    sum_beside(1, at.cross).start()
    sum_beside(0, at.near).start()
    order = list(range(strips - 1, -1, -1))
    for k in order:
        beside(k, 1, at.cross).start()
        beside(k, 0, at.near).start()

    sum_beside(1, at.cross).wait_recv()
    sum_far[...] = sums_ref[:, sum_rows(at.far)] + sum_near[1]
    sum_across.start()
    for k in order:
        beside(k, 1, at.cross).wait_recv()
        far_out[k] = stacked_ref[:, rows(k, at.far)] + near_land[k, 1]
        across(k).start()
    sum_beside(0, at.near).wait_recv()
    total = sums_ref[:, sum_rows(at.own)] + sum_near[0]
    sum_across.wait_recv()
    sum_steps[0] = total + sum_land[...]
    if steps:
        step(0).start()
    for k in order:
        beside(k, 0, at.near).wait_recv()
        across(k).wait_recv()
        kept[k] = stacked_ref[:, rows(k, at.own)] + near_land[k, 0] + far_land[k]
        if k < strips - 1:
            @pl.when(at.tile > 0)
            def _(k=k):
                down(k + 1).wait_recv()
                kept[k] += rim_land[k]

        if k > 0:
            @pl.when(at.tile < at.tiles - 1)
            def _(k=k):
                down(k).start()

        i = strips - 1 - k
        if i < min(steps, strips - 1):
            step(i).wait_recv()
            sum_steps[i + 1] = sum_steps[i] + step_land[i]
            if i + 1 < steps:
                step(i + 1).start()
    for i in range(min(steps, strips - 1), steps):
        step(i).wait_recv()
        sum_steps[i + 1] = sum_steps[i] + step_land[i]
        if i + 1 < steps:
            step(i + 1).start()

    def out(ref, which, lane, quarter, count, peer):
        place = ref.at[:, at.rows(0, quarter, count)]
        return remote(place, place, out_send.at[which, lane], out_recv.at[which, lane], peer)

    probe_ref[:, sum_rows(at.own)] = (
        -PROBE_RATE * sum_steps[steps, : 2 * (sums_ref.shape[0] // 2)] / (sum_steps[steps, 2 * (sums_ref.shape[0] // 2)] + RELAX)
    )
    outs = [(probe_ref, 0, sum_part), (object_ref, 1, part)]
    ref, which, count = outs[0]
    out(ref, which, 0, at.own, count, at.far_id).start()
    out(ref, which, 1, at.own, count, at.near_id).start()
    object_ref[:, rows(0, at.own)] = -kept[0, :planes] / (kept[0, planes] + RELAX)
    ref, which, count = outs[1]
    out(ref, which, 0, at.own, count, at.far_id).start()
    out(ref, which, 1, at.own, count, at.near_id).start()
    for ref, which, count in outs:
        out(ref, which, 0, at.far, count, at.far_id).wait_recv()
        out(ref, which, 2, at.far, count, at.near_id).start()
    for ref, which, count in outs:
        out(ref, which, 1, at.near, count, at.near_id).wait_recv()
        out(ref, which, 2, at.cross, count, at.near_id).wait_recv()
        out(ref, which, 0, at.own, count, at.far_id).wait_send()
        out(ref, which, 1, at.own, count, at.near_id).wait_send()
        out(ref, which, 2, at.far, count, at.near_id).wait_send()

    sum_beside(1, at.cross).wait_send()
    sum_beside(0, at.near).wait_send()
    sum_across.wait_send()
    for k in order:
        beside(k, 1, at.cross).wait_send()
        beside(k, 0, at.near).wait_send()
        across(k).wait_send()
        if k > 0:
            @pl.when(at.tile < at.tiles - 1)
            def _(k=k):
                down(k).wait_send()
    for i in range(steps):
        step(i).wait_send()


def reduced(stacked, sums, strip, tiles, replicas):
    planes, ext_rows, width = stacked.shape
    strips = ext_rows // strip
    part = strip // replicas
    sum_planes, side, _ = sums.shape
    sum_part = side // replicas
    steps = tiles.bit_length() - 1
    vmem = pl.BlockSpec(memory_space=pltpu.VMEM)
    dma = pltpu.SemaphoreType.DMA
    block = (planes, part, width)
    sum_block = (sum_planes, sum_part, side)

    def buffer(*shape):
        return pltpu.VMEM(shape, jnp.float32)

    return pl.pallas_call(
        reduce_kernel,
        out_shape=(
            jax.ShapeDtypeStruct((planes - 1, strip, width), jnp.float32),
            jax.ShapeDtypeStruct((sum_planes - 1, side, side), jnp.float32),
        ),
        in_specs=[vmem, vmem],
        out_specs=(vmem, vmem),
        scratch_shapes=[
            buffer(strips, 2, *block),
            buffer(strips, *block),
            buffer(strips, *block),
            buffer(strips, *block),
            buffer(strips - 1, *block),
            buffer(2, *sum_block),
            buffer(*sum_block),
            buffer(*sum_block),
            buffer(steps + 1, *sum_block),
            buffer(max(steps, 1), *sum_block),
            dma((strips, 2)), dma((strips, 2)), dma((strips,)), dma((strips,)), dma((strips - 1,)), dma((strips - 1,)),
            dma((2,)), dma((2,)), dma, dma, dma((max(steps, 1),)), dma((max(steps, 1),)), dma((2, 3)), dma((2, 3)),
        ],
        compiler_params=pltpu.CompilerParams(
            collective_id=1, has_side_effects=True, vmem_limit_bytes=48 * MIB
        ),
        name="reduce",
    )(stacked, sums)


def per_device(object_field, probe_modes, measured, row_offset, col_offset, position_count):
    layers, _, strip_rows, width = object_field.shape
    side = probe_modes.shape[2]
    reach = side // strip_rows
    tiles = lax.axis_size("tile")
    replicas = lax.axis_size("pos")
    own = object_field.reshape(2 * layers, strip_rows, width)
    slots_here = row_offset.size
    count = jnp.broadcast_to(position_count.reshape(1, 1), (1, slots_here))
    info = jnp.concatenate(
        [row_offset.reshape(1, -1), col_offset.reshape(1, -1), count], axis=0
    )
    info = jnp.pad(info, ((0, 5), (0, 128 - slots_here)))
    extended, info_pair, measured_pair = halo(own, info, measured.reshape(-1, side, side), reach)
    stacked, sums = slots(info_pair, extended, probe_modes, measured_pair)
    object_flat, probe_flat = reduced(stacked, sums, strip_rows, tiles, replicas)
    return object_flat.reshape(object_field.shape), probe_flat.reshape(probe_modes.shape)


def solution(mesh):
    return jax.shard_map(
        per_device,
        mesh=mesh,
        in_specs=(
            P("groups", None, "tile", None),
            P("groups", None, None, None),
            P(("groups", "tile"), "pos", None, None, None),
            P(("groups", "tile"), "pos", None),
            P(("groups", "tile"), "pos", None),
            P(("groups", "tile"), "pos"),
        ),
        out_specs=(P("groups", None, "tile", None), P("groups", None, None, None)),
        check_vma=False,
    )
```

```python
import functools
import math

import jax
import jax.numpy as jnp
import numpy as np
from jax import lax
from jax.experimental import pallas as pl
from jax.experimental.pallas import tpu as pltpu
from jax.sharding import PartitionSpec as P

FRESNEL = 0.25
RELAX = 1.0
PROBE_RATE = 4.0
MIB = 1024 * 1024
CUTS = 2


def block_tables(side):
    indices = np.arange(side)
    angle = 2.0 * np.pi / side * (indices[:, None] * indices[None, :] % side)
    fourier = np.exp(-1j * angle) / np.sqrt(side)
    frequency = np.where(indices < side // 2, indices, indices - side) / side
    kernel = np.exp(-1j * math.pi * FRESNEL * side * frequency * frequency)
    propagator = (np.conj(fourier) * kernel[None, :]) @ fourier
    blocks = []
    for table in (propagator, np.conj(propagator), fourier, np.conj(fourier)):
        blocks.append(np.block([[table.real, table.imag], [-table.imag, table.real]]))
    stacked = np.stack(blocks).astype(np.float32)
    high = stacked.astype(jnp.bfloat16)
    low = (stacked - high.astype(np.float32)).astype(jnp.bfloat16)
    return high, low


def halves(value):
    high = value.astype(jnp.bfloat16)
    low = (value - high.astype(jnp.float32)).astype(jnp.bfloat16)
    return high, low


def dot(left, right):
    return jnp.dot(left, right, preferred_element_type=jnp.float32)


def both_sides(fields, right_high, right_low, left_high, left_low):
    side = fields[0][0].shape[0]
    rows = jnp.concatenate([jnp.concatenate(field, axis=1) for field in fields], axis=0)
    high, low = halves(rows)
    half = dot(high, right_high) + dot(high, right_low) + dot(low, right_high)
    tops = [half[i * side : (i + 1) * side, :side] for i in range(len(fields))]
    ends = [half[i * side : (i + 1) * side, side:] for i in range(len(fields))]
    cols = jnp.concatenate([jnp.concatenate(tops, axis=1), jnp.concatenate(ends, axis=1)], axis=0)
    high, low = halves(cols)
    done = dot(left_high, high) + dot(left_low, high) + dot(left_high, low)
    return [
        (done[:side, i * side : (i + 1) * side], done[side:, i * side : (i + 1) * side])
        for i in range(len(fields))
    ]


def times(left, right):
    return (left[0] * right[0] - left[1] * right[1], left[0] * right[1] + left[1] * right[0])


def times_conj(left, right):
    return (left[0] * right[0] + left[1] * right[1], left[1] * right[0] - left[0] * right[1])


def slots_kernel(
    info_ref, object_ref, probe_ref, measured_ref, high_ref, low_ref,
    stacked_ref, sums_ref, light_ref, mid_ref, far_ref,
):
    modes, _, side, _ = probe_ref.shape
    width = object_ref.shape[2]
    stacked_ref[...] = jnp.zeros_like(stacked_ref)
    sums_ref[...] = jnp.zeros_like(sums_ref)
    light = jnp.zeros((side, side), jnp.float32)
    for m in range(modes):
        light = light + probe_ref[m, 0] * probe_ref[m, 0] + probe_ref[m, 1] * probe_ref[m, 1]
    light_ref[...] = light
    groups = [list(range(modes))]
    prop, prop_c, four, four_c = range(4)

    def apply(fields, table, conj_table):
        return both_sides(
            fields, high_ref[table], low_ref[table], high_ref[conj_table], low_ref[conj_table]
        )

    parity = lax.rem(lax.axis_index("pos"), 2)
    count_even = info_ref[0, 2, 0]
    count_all = count_even + info_ref[1, 2, 0]
    half = (count_all + 1) // 2
    first_slot = parity * half
    last_slot = jnp.where(parity == 0, half, count_all)

    def visit(slot, carry):
        second = (slot >= count_even).astype(jnp.int32)
        within = slot - second * count_even
        row = info_ref[second, 0, within]
        col = info_ref[second, 1, within]
        base = pl.multiple_of(jnp.minimum(col // 128 * 128, width - 2 * 128), 128)
        offset = col - base
        lane = lax.broadcasted_iota(jnp.int32, (side + 8, 128), 1)
        back = lax.rem(128 - lax.rem(offset, 128), 128)
        ahead = lax.rem(offset, 128)

        start = pl.multiple_of(row // 8 * 8, 8)
        shift = row - start
        tall = side + 8
        rise = lax.rem(tall - shift, tall)

        def patch(plane):
            left = object_ref[plane, pl.ds(start, tall), pl.ds(base, 128)]
            right = object_ref[plane, pl.ds(start, tall), pl.ds(base + 128, 128)]
            chosen = pltpu.roll(jnp.where(lane >= offset, left, right), back, 1)
            return pltpu.roll(chosen, rise, 0)[:side]

        def place(plane, value):
            value = jnp.concatenate([value, jnp.zeros((8, side), jnp.float32)], axis=0)
            value = pltpu.roll(pltpu.roll(value, ahead, 1), shift, 0)
            kept = lane >= offset
            left = jnp.where(kept, value, 0.0)
            right = jnp.where(kept, 0.0, value)
            at = (plane, pl.ds(start, tall), pl.ds(base, 128))
            stacked_ref[at] = stacked_ref[at] + left
            at = (plane, pl.ds(start, tall), pl.ds(base + 128, 128))
            stacked_ref[at] = stacked_ref[at] + right

        upper = (patch(0), patch(1))
        lower = (patch(2), patch(3))
        sums_ref[2 * modes] += upper[0] * upper[0] + upper[1] * upper[1]
        place(4, light_ref[...])
        intensity = jnp.zeros((side, side), jnp.float32)
        for group in groups:
            waves = [times((probe_ref[m, 0], probe_ref[m, 1]), upper) for m in group]
            waves = apply(waves, prop, prop_c)
            for m, wave in zip(group, waves):
                mid_ref[m, 0] = wave[0]
                mid_ref[m, 1] = wave[1]
            waves = apply([times(wave, lower) for wave in waves], four, four_c)
            for m, wave in zip(group, waves):
                far_ref[m, 0] = wave[0]
                far_ref[m, 1] = wave[1]
                intensity = intensity + wave[0] * wave[0] + wave[1] * wave[1]
        misfit = 2.0 * (intensity - measured_ref[second, within])
        zero = jnp.zeros((side, side), jnp.float32)
        lower_grad = (zero, zero)
        upper_grad = (zero, zero)
        for group in groups:
            grads = [(misfit * far_ref[m, 0], misfit * far_ref[m, 1]) for m in group]
            grads = apply(grads, four_c, four)
            for m, grad in zip(group, grads):
                term = times_conj(grad, (mid_ref[m, 0], mid_ref[m, 1]))
                lower_grad = (lower_grad[0] + term[0], lower_grad[1] + term[1])
            grads = apply([times_conj(grad, lower) for grad in grads], prop_c, prop)
            for m, grad in zip(group, grads):
                term = times_conj(grad, (probe_ref[m, 0], probe_ref[m, 1]))
                upper_grad = (upper_grad[0] + term[0], upper_grad[1] + term[1])
                term = times_conj(grad, upper)
                sums_ref[2 * m] += term[0]
                sums_ref[2 * m + 1] += term[1]
        place(0, upper_grad[0])
        place(1, upper_grad[1])
        place(2, lower_grad[0])
        place(3, lower_grad[1])
        return carry

    lax.fori_loop(first_slot, last_slot, visit, 0)


def slots(info, extended, probe_modes, measured):
    modes, _, side, _ = probe_modes.shape
    high, low = block_tables(side)
    planes, ext_rows, width = extended.shape
    vmem = pl.BlockSpec(memory_space=pltpu.VMEM)
    smem = pl.BlockSpec(memory_space=pltpu.SMEM)
    return pl.pallas_call(
        slots_kernel,
        out_shape=(
            jax.ShapeDtypeStruct((planes + 1, ext_rows, width), jnp.float32),
            jax.ShapeDtypeStruct((2 * modes + 1, side, side), jnp.float32),
        ),
        in_specs=[smem] + [vmem] * 5,
        out_specs=(vmem,) * 2,
        scratch_shapes=[
            pltpu.VMEM((side, side), jnp.float32),
            pltpu.VMEM(probe_modes.shape, jnp.float32),
            pltpu.VMEM(probe_modes.shape, jnp.float32),
        ],
        compiler_params=pltpu.CompilerParams(vmem_limit_bytes=40 * MIB),
        name="slots",
    )(info, extended, probe_modes, measured, jnp.asarray(high), jnp.asarray(low))


def flipped(index, bit):
    return index + bit - 2 * bit * (index // bit % 2)


def greet(peers):
    barrier = pltpu.get_barrier_semaphore()
    for peer in peers:
        pl.semaphore_signal(barrier, inc=1, device_id=peer, device_id_type=pl.DeviceIdType.MESH)
    pl.semaphore_wait(barrier, len(peers))


def remote(source, target, send_sem, recv_sem, peer):
    return pltpu.make_async_remote_copy(
        src_ref=source,
        dst_ref=target,
        send_sem=send_sem,
        recv_sem=recv_sem,
        device_id=peer,
        device_id_type=pl.DeviceIdType.MESH,
    )


class Places:
    def __init__(self):
        self.tiles = lax.axis_size("tile")
        self.replicas = lax.axis_size("pos")
        self.tile = lax.axis_index("tile")
        self.own = lax.axis_index("pos")
        self.near = flipped(self.own, 1)
        self.far = flipped(self.own, 2)
        self.cross = flipped(self.near, 2)
        self.near_id = {"pos": self.near}
        self.far_id = {"pos": self.far}
        self.up_id = {"tile": lax.rem(self.tile + self.tiles - 1, self.tiles)}
        self.down_id = {"tile": lax.rem(self.tile + 1, self.tiles)}

    def rows(self, first, quarter, count):
        return pl.ds(pl.multiple_of(first + quarter * count, 8), count)


def halo_kernel(
    own_ref, info_ref, measured_ref, ext_ref, info_pair, measured_pair,
    tile_send, tile_recv, far_send, far_recv, near_send, near_recv, pair_send, pair_recv,
):
    at = Places()
    strip = own_ref.shape[1]
    part = strip // at.replicas
    reach = ext_ref.shape[1] // strip - 1
    greet([at.near_id, at.far_id, at.up_id, at.down_id])

    def cols(j):
        piece = own_ref.shape[2] // CUTS
        return pl.ds(j * piece, piece)

    def slot(k, j, quarter):
        return ext_ref.at[:, at.rows(k * strip, quarter, part), cols(j)]

    def up(k, j):
        i = (k - 1) * CUTS + j
        if k == 1:
            source = own_ref.at[:, at.rows(0, at.own, part), cols(j)]
        else:
            source = slot(k - 1, j, at.own)
        return remote(source, slot(k, j, at.own), tile_send.at[i], tile_recv.at[i], at.up_id)

    def across(k, j, quarter):
        i = (k - 1) * CUTS + j
        place = slot(k, j, quarter)
        return remote(place, place, far_send.at[i], far_recv.at[i], at.far_id)

    def beside(k, j, which, quarter):
        i = (k - 1) * CUTS + j
        place = slot(k, j, quarter)
        return remote(place, place, near_send.at[i, which], near_recv.at[i, which], at.near_id)

    def sends(k):
        return jnp.logical_and(at.tile > 0, at.tile + k - 1 < at.tiles)

    @pl.when(sends(1))
    def _():
        for j in range(CUTS):
            up(1, j).start()

    parity = lax.rem(at.own, 2)

    def share(i, place):
        source = (info_ref, measured_ref)[i]
        pair = (info_pair, measured_pair)[i]
        return remote(source, pair.at[place], pair_send.at[i], pair_recv.at[i], at.near_id)

    share(0, parity).start()
    share(1, parity).start()
    info_pair[parity] = info_ref[...]
    measured_pair[parity] = measured_ref[...]
    ext_ref[:, :strip] = own_ref[...]
    for k in range(1, reach + 1):
        @pl.when(at.tile + k >= at.tiles)
        def _(k=k):
            ext_ref[:, k * strip : (k + 1) * strip] = jnp.zeros(own_ref.shape, jnp.float32)

    items = [(k, j) for k in range(1, reach + 1) for j in range(CUTS)]

    def second_hop(k, j):
        @pl.when(at.tile + k < at.tiles)
        def _():
            across(k, j, at.far).wait_recv()
            beside(k, j, 1, at.far).start()

    for i, (k, j) in enumerate(items):
        @pl.when(at.tile + k < at.tiles)
        def _(k=k, j=j):
            up(k, j).wait_recv()

        if k < reach:
            @pl.when(sends(k + 1))
            def _(k=k, j=j):
                up(k + 1, j).start()

        @pl.when(at.tile + k < at.tiles)
        def _(k=k, j=j):
            across(k, j, at.own).start()
            beside(k, j, 0, at.own).start()

        if i > 0:
            second_hop(*items[i - 1])
    second_hop(*items[-1])

    for k, j in items:
        @pl.when(sends(k))
        def _(k=k, j=j):
            up(k, j).wait_send()

        @pl.when(at.tile + k < at.tiles)
        def _(k=k, j=j):
            beside(k, j, 0, at.near).wait_recv()
            beside(k, j, 1, at.cross).wait_recv()
            across(k, j, at.own).wait_send()
            beside(k, j, 0, at.own).wait_send()
            beside(k, j, 1, at.far).wait_send()

    for i in range(2):
        share(i, 1 - parity).wait_recv()
        share(i, parity).wait_send()


def halo(own, info, measured, reach):
    planes, strip, width = own.shape
    vmem = pl.BlockSpec(memory_space=pltpu.VMEM)
    dma = pltpu.SemaphoreType.DMA
    return pl.pallas_call(
        halo_kernel,
        out_shape=(
            jax.ShapeDtypeStruct((planes, strip * (reach + 1), width), jnp.float32),
            jax.ShapeDtypeStruct((2,) + info.shape, jnp.int32),
            jax.ShapeDtypeStruct((2,) + measured.shape, jnp.float32),
        ),
        in_specs=[vmem] * 3,
        out_specs=(vmem,) * 3,
        scratch_shapes=[
            *[dma((reach * CUTS,))] * 4, *[dma((reach * CUTS, 2))] * 2,
            dma((2,)), dma((2,)),
        ],
        compiler_params=pltpu.CompilerParams(
            collective_id=0, has_side_effects=True, vmem_limit_bytes=40 * MIB
        ),
        name="halo",
    )(own, info, measured)


def reduce_kernel(
    stacked_ref, sums_ref, object_ref, probe_ref,
    near_land, far_out, far_land, kept, rim_land, sum_near, sum_far, sum_land, sum_steps, step_land,
    near_send, near_recv, far_send, far_recv, rim_send, rim_recv,
    pn_send, pn_recv, pf_send, pf_recv, step_send, step_recv, out_send, out_recv,
):
    at = Places()
    strip = object_ref.shape[1]
    part = strip // at.replicas
    planes = object_ref.shape[0]
    strips = stacked_ref.shape[1] // strip
    sum_part = sums_ref.shape[1] // at.replicas
    steps = at.tiles.bit_length() - 1
    partners = [{"tile": flipped(at.tile, 2**i)} for i in range(steps)]
    greet([at.near_id, at.far_id, at.up_id, at.down_id] + partners)

    def rows(k, quarter):
        return at.rows(k * strip, quarter, part)

    def sum_rows(quarter):
        return at.rows(0, quarter, sum_part)

    def sum_beside(which, quarter):
        return remote(
            sums_ref.at[:, sum_rows(quarter)], sum_near.at[which], pn_send.at[which], pn_recv.at[which], at.near_id
        )

    width = stacked_ref.shape[2]

    def cols(j):
        return pl.ds(j * (width // CUTS), width // CUTS)

    def beside(k, j, which, quarter):
        return remote(
            stacked_ref.at[:, rows(k, quarter), cols(j)], near_land.at[k, j, which],
            near_send.at[k, j, which], near_recv.at[k, j, which], at.near_id,
        )

    def across(k, j):
        return remote(
            far_out.at[k, j], far_land.at[k, j], far_send.at[k, j], far_recv.at[k, j], at.far_id
        )

    def down(k, j):
        return remote(
            kept.at[k, j], rim_land.at[k - 1, j], rim_send.at[k - 1, j], rim_recv.at[k - 1, j], at.down_id
        )

    def step(i):
        return remote(sum_steps.at[i], step_land.at[i], step_send.at[i], step_recv.at[i], partners[i])

    def object_out(j, lane, quarter, peer):
        place = object_ref.at[:, rows(0, quarter), cols(j)]
        return remote(place, place, out_send.at[1 + j, lane], out_recv.at[1 + j, lane], peer)

    def probe_out(lane, quarter, peer):
        place = probe_ref.at[:, sum_rows(quarter)]
        return remote(place, place, out_send.at[0, lane], out_recv.at[0, lane], peer)

    def probe_update():
        last = sums_ref.shape[0] - 1
        update = -PROBE_RATE * sum_steps[steps, :last] / (sum_steps[steps, last] + RELAX)
        probe_ref[:, sum_rows(at.own)] = update
        probe_out(0, at.own, at.far_id).start()
        probe_out(1, at.own, at.near_id).start()

    sum_across = remote(sum_far, sum_land, pf_send, pf_recv, at.far_id)

    sum_beside(1, at.cross).start()
    sum_beside(0, at.near).start()
    order = [(k, j) for k in range(strips - 1, -1, -1) for j in range(CUTS)]
    for k, j in order:
        beside(k, j, 1, at.cross).start()
    for k, j in order:
        beside(k, j, 0, at.near).start()

    sum_beside(1, at.cross).wait_recv()
    sum_far[...] = sums_ref[:, sum_rows(at.far)] + sum_near[1]
    sum_across.start()
    for k, j in order:
        beside(k, j, 1, at.cross).wait_recv()
        far_out[k, j] = stacked_ref[:, rows(k, at.far), cols(j)] + near_land[k, j, 1]
        across(k, j).start()
    sum_beside(0, at.near).wait_recv()
    total = sums_ref[:, sum_rows(at.own)] + sum_near[0]
    sum_across.wait_recv()
    sum_steps[0] = total + sum_land[...]
    if steps:
        step(0).start()
    for k, j in order:
        beside(k, j, 0, at.near).wait_recv()
        across(k, j).wait_recv()
        kept[k, j] = stacked_ref[:, rows(k, at.own), cols(j)] + near_land[k, j, 0] + far_land[k, j]
        if k < strips - 1:
            @pl.when(at.tile > 0)
            def _(k=k, j=j):
                down(k + 1, j).wait_recv()
                kept[k, j] += rim_land[k, j]

        if k > 0:
            @pl.when(at.tile < at.tiles - 1)
            def _(k=k, j=j):
                down(k, j).start()
        else:
            update = -kept[0, j, :planes] / (kept[0, j, planes] + RELAX)
            object_ref[:, rows(0, at.own), cols(j)] = update
            object_out(j, 0, at.own, at.far_id).start()
            object_out(j, 1, at.own, at.near_id).start()

        i = strips - 1 - k
        if j == CUTS - 1 and i < min(steps, strips - 1):
            step(i).wait_recv()
            sum_steps[i + 1] = sum_steps[i] + step_land[i]
            if i + 1 < steps:
                step(i + 1).start()
            elif i + 1 == steps:
                probe_update()
    for i in range(min(steps, strips - 1), steps):
        step(i).wait_recv()
        sum_steps[i + 1] = sum_steps[i] + step_land[i]
        if i + 1 < steps:
            step(i + 1).start()

    if steps > strips - 1 or steps == 0:
        probe_update()
    outs = [probe_out] + [functools.partial(object_out, j) for j in range(CUTS)]
    for out in outs:
        out(0, at.far, at.far_id).wait_recv()
        out(2, at.far, at.near_id).start()
    for out in outs:
        out(1, at.near, at.near_id).wait_recv()
        out(2, at.cross, at.near_id).wait_recv()
        out(0, at.own, at.far_id).wait_send()
        out(1, at.own, at.near_id).wait_send()
        out(2, at.far, at.near_id).wait_send()

    sum_beside(1, at.cross).wait_send()
    sum_beside(0, at.near).wait_send()
    sum_across.wait_send()
    for k, j in order:
        beside(k, j, 1, at.cross).wait_send()
        beside(k, j, 0, at.near).wait_send()
        across(k, j).wait_send()
        if k > 0:
            @pl.when(at.tile < at.tiles - 1)
            def _(k=k, j=j):
                down(k, j).wait_send()
    for i in range(steps):
        step(i).wait_send()


def reduced(stacked, sums, strip, tiles, replicas):
    planes, ext_rows, width = stacked.shape
    strips = ext_rows // strip
    part = strip // replicas
    sum_planes, side, _ = sums.shape
    sum_part = side // replicas
    steps = tiles.bit_length() - 1
    vmem = pl.BlockSpec(memory_space=pltpu.VMEM)
    dma = pltpu.SemaphoreType.DMA
    block = (planes, part, width // CUTS)
    sum_block = (sum_planes, sum_part, side)

    def buffer(*shape):
        return pltpu.VMEM(shape, jnp.float32)

    return pl.pallas_call(
        reduce_kernel,
        out_shape=(
            jax.ShapeDtypeStruct((planes - 1, strip, width), jnp.float32),
            jax.ShapeDtypeStruct((sum_planes - 1, side, side), jnp.float32),
        ),
        in_specs=[vmem, vmem],
        out_specs=(vmem, vmem),
        scratch_shapes=[
            buffer(strips, CUTS, 2, *block),
            buffer(strips, CUTS, *block),
            buffer(strips, CUTS, *block),
            buffer(strips, CUTS, *block),
            buffer(strips - 1, CUTS, *block),
            buffer(2, *sum_block),
            buffer(*sum_block),
            buffer(*sum_block),
            buffer(steps + 1, *sum_block),
            buffer(max(steps, 1), *sum_block),
            *[dma((strips, CUTS, 2))] * 2, *[dma((strips, CUTS))] * 2, *[dma((strips - 1, CUTS))] * 2,
            dma((2,)), dma((2,)), dma, dma, dma((max(steps, 1),)), dma((max(steps, 1),)), *[dma((1 + CUTS, 3))] * 2,
        ],
        compiler_params=pltpu.CompilerParams(
            collective_id=1, has_side_effects=True, vmem_limit_bytes=48 * MIB
        ),
        name="reduce",
    )(stacked, sums)


def per_device(object_field, probe_modes, measured, row_offset, col_offset, position_count):
    layers, _, strip_rows, width = object_field.shape
    side = probe_modes.shape[2]
    reach = side // strip_rows
    tiles = lax.axis_size("tile")
    replicas = lax.axis_size("pos")
    own = object_field.reshape(2 * layers, strip_rows, width)
    slots_here = row_offset.size
    count = jnp.broadcast_to(position_count.reshape(1, 1), (1, slots_here))
    info = jnp.concatenate(
        [row_offset.reshape(1, -1), col_offset.reshape(1, -1), count], axis=0
    )
    info = jnp.pad(info, ((0, 5), (0, 128 - slots_here)))
    extended, info_pair, measured_pair = halo(own, info, measured.reshape(-1, side, side), reach)
    stacked, sums = slots(info_pair, extended, probe_modes, measured_pair)
    object_flat, probe_flat = reduced(stacked, sums, strip_rows, tiles, replicas)
    return object_flat.reshape(object_field.shape), probe_flat.reshape(probe_modes.shape)


def solution(mesh):
    return jax.shard_map(
        per_device,
        mesh=mesh,
        in_specs=(
            P("groups", None, "tile", None),
            P("groups", None, None, None),
            P(("groups", "tile"), "pos", None, None, None),
            P(("groups", "tile"), "pos", None),
            P(("groups", "tile"), "pos", None),
            P(("groups", "tile"), "pos"),
        ),
        out_specs=(P("groups", None, "tile", None), P("groups", None, None, None)),
        check_vma=False,
    )
```

```python
import functools
import math

import jax
import jax.numpy as jnp
import numpy as np
from jax import lax
from jax.experimental import pallas as pl
from jax.experimental.pallas import tpu as pltpu
from jax.sharding import PartitionSpec as P

FRESNEL = 0.25
RELAX = 1.0
PROBE_RATE = 4.0
MIB = 1024 * 1024
CUTS = 4


def block_tables(side):
    indices = np.arange(side)
    angle = 2.0 * np.pi / side * (indices[:, None] * indices[None, :] % side)
    fourier = np.exp(-1j * angle) / np.sqrt(side)
    frequency = np.where(indices < side // 2, indices, indices - side) / side
    kernel = np.exp(-1j * math.pi * FRESNEL * side * frequency * frequency)
    propagator = (np.conj(fourier) * kernel[None, :]) @ fourier
    blocks = []
    for table in (propagator, np.conj(propagator), fourier, np.conj(fourier)):
        blocks.append(np.block([[table.real, table.imag], [-table.imag, table.real]]))
    stacked = np.stack(blocks).astype(np.float32)
    high = stacked.astype(jnp.bfloat16)
    low = (stacked - high.astype(np.float32)).astype(jnp.bfloat16)
    return high, low


def halves(value):
    high = value.astype(jnp.bfloat16)
    low = (value - high.astype(jnp.float32)).astype(jnp.bfloat16)
    return high, low


def dot(left, right):
    return jnp.dot(left, right, preferred_element_type=jnp.float32)


def both_sides(fields, right_high, right_low, left_high, left_low):
    side = fields[0][0].shape[0]
    rows = jnp.concatenate([jnp.concatenate(field, axis=1) for field in fields], axis=0)
    high, low = halves(rows)
    half = dot(high, right_high) + dot(high, right_low) + dot(low, right_high)
    tops = [half[i * side : (i + 1) * side, :side] for i in range(len(fields))]
    ends = [half[i * side : (i + 1) * side, side:] for i in range(len(fields))]
    cols = jnp.concatenate([jnp.concatenate(tops, axis=1), jnp.concatenate(ends, axis=1)], axis=0)
    high, low = halves(cols)
    done = dot(left_high, high) + dot(left_low, high) + dot(left_high, low)
    return [
        (done[:side, i * side : (i + 1) * side], done[side:, i * side : (i + 1) * side])
        for i in range(len(fields))
    ]


def times(left, right):
    return (left[0] * right[0] - left[1] * right[1], left[0] * right[1] + left[1] * right[0])


def times_conj(left, right):
    return (left[0] * right[0] + left[1] * right[1], left[1] * right[0] - left[0] * right[1])


def slots_kernel(
    info_ref, object_ref, probe_ref, measured_ref, high_ref, low_ref,
    stacked_ref, sums_ref, light_ref, mid_ref, far_ref,
):
    modes, _, side, _ = probe_ref.shape
    width = object_ref.shape[2]
    stacked_ref[...] = jnp.zeros_like(stacked_ref)
    sums_ref[...] = jnp.zeros_like(sums_ref)
    light = jnp.zeros((side, side), jnp.float32)
    for m in range(modes):
        light = light + probe_ref[m, 0] * probe_ref[m, 0] + probe_ref[m, 1] * probe_ref[m, 1]
    light_ref[...] = light
    groups = [list(range(modes))]
    prop, prop_c, four, four_c = range(4)

    def apply(fields, table, conj_table):
        return both_sides(
            fields, high_ref[table], low_ref[table], high_ref[conj_table], low_ref[conj_table]
        )

    parity = lax.rem(lax.axis_index("pos"), 2)
    count_even = info_ref[0, 2, 0]
    count_all = count_even + info_ref[1, 2, 0]
    half = (count_all + 1) // 2
    first_slot = parity * half
    last_slot = jnp.where(parity == 0, half, count_all)

    def visit(slot, carry):
        second = (slot >= count_even).astype(jnp.int32)
        within = slot - second * count_even
        row = info_ref[second, 0, within]
        col = info_ref[second, 1, within]
        base = pl.multiple_of(jnp.minimum(col // 128 * 128, width - 2 * 128), 128)
        offset = col - base
        lane = lax.broadcasted_iota(jnp.int32, (side + 8, 128), 1)
        back = lax.rem(128 - lax.rem(offset, 128), 128)
        ahead = lax.rem(offset, 128)

        start = pl.multiple_of(row // 8 * 8, 8)
        shift = row - start
        tall = side + 8
        rise = lax.rem(tall - shift, tall)

        def patch(plane):
            left = object_ref[plane, pl.ds(start, tall), pl.ds(base, 128)]
            right = object_ref[plane, pl.ds(start, tall), pl.ds(base + 128, 128)]
            chosen = pltpu.roll(jnp.where(lane >= offset, left, right), back, 1)
            return pltpu.roll(chosen, rise, 0)[:side]

        def place(plane, value):
            value = jnp.concatenate([value, jnp.zeros((8, side), jnp.float32)], axis=0)
            value = pltpu.roll(pltpu.roll(value, ahead, 1), shift, 0)
            kept = lane >= offset
            left = jnp.where(kept, value, 0.0)
            right = jnp.where(kept, 0.0, value)
            at = (plane, pl.ds(start, tall), pl.ds(base, 128))
            stacked_ref[at] = stacked_ref[at] + left
            at = (plane, pl.ds(start, tall), pl.ds(base + 128, 128))
            stacked_ref[at] = stacked_ref[at] + right

        upper = (patch(0), patch(1))
        lower = (patch(2), patch(3))
        sums_ref[2 * modes] += upper[0] * upper[0] + upper[1] * upper[1]
        place(4, light_ref[...])
        intensity = jnp.zeros((side, side), jnp.float32)
        for group in groups:
            waves = [times((probe_ref[m, 0], probe_ref[m, 1]), upper) for m in group]
            waves = apply(waves, prop, prop_c)
            for m, wave in zip(group, waves):
                mid_ref[m, 0] = wave[0]
                mid_ref[m, 1] = wave[1]
            waves = apply([times(wave, lower) for wave in waves], four, four_c)
            for m, wave in zip(group, waves):
                far_ref[m, 0] = wave[0]
                far_ref[m, 1] = wave[1]
                intensity = intensity + wave[0] * wave[0] + wave[1] * wave[1]
        misfit = 2.0 * (intensity - measured_ref[second, within])
        zero = jnp.zeros((side, side), jnp.float32)
        lower_grad = (zero, zero)
        upper_grad = (zero, zero)
        for group in groups:
            grads = [(misfit * far_ref[m, 0], misfit * far_ref[m, 1]) for m in group]
            grads = apply(grads, four_c, four)
            for m, grad in zip(group, grads):
                term = times_conj(grad, (mid_ref[m, 0], mid_ref[m, 1]))
                lower_grad = (lower_grad[0] + term[0], lower_grad[1] + term[1])
            grads = apply([times_conj(grad, lower) for grad in grads], prop_c, prop)
            for m, grad in zip(group, grads):
                term = times_conj(grad, (probe_ref[m, 0], probe_ref[m, 1]))
                upper_grad = (upper_grad[0] + term[0], upper_grad[1] + term[1])
                term = times_conj(grad, upper)
                sums_ref[2 * m] += term[0]
                sums_ref[2 * m + 1] += term[1]
        place(0, upper_grad[0])
        place(1, upper_grad[1])
        place(2, lower_grad[0])
        place(3, lower_grad[1])
        return carry

    lax.fori_loop(first_slot, last_slot, visit, 0)


def slots(info, extended, probe_modes, measured):
    modes, _, side, _ = probe_modes.shape
    high, low = block_tables(side)
    planes, ext_rows, width = extended.shape
    vmem = pl.BlockSpec(memory_space=pltpu.VMEM)
    smem = pl.BlockSpec(memory_space=pltpu.SMEM)
    return pl.pallas_call(
        slots_kernel,
        out_shape=(
            jax.ShapeDtypeStruct((planes + 1, ext_rows, width), jnp.float32),
            jax.ShapeDtypeStruct((2 * modes + 1, side, side), jnp.float32),
        ),
        in_specs=[smem] + [vmem] * 5,
        out_specs=(vmem,) * 2,
        scratch_shapes=[
            pltpu.VMEM((side, side), jnp.float32),
            pltpu.VMEM(probe_modes.shape, jnp.float32),
            pltpu.VMEM(probe_modes.shape, jnp.float32),
        ],
        compiler_params=pltpu.CompilerParams(vmem_limit_bytes=40 * MIB),
        name="slots",
    )(info, extended, probe_modes, measured, jnp.asarray(high), jnp.asarray(low))


def flipped(index, bit):
    return index + bit - 2 * bit * (index // bit % 2)


def greet(peers):
    barrier = pltpu.get_barrier_semaphore()
    for peer in peers:
        pl.semaphore_signal(barrier, inc=1, device_id=peer, device_id_type=pl.DeviceIdType.MESH)
    pl.semaphore_wait(barrier, len(peers))


def remote(source, target, send_sem, recv_sem, peer):
    return pltpu.make_async_remote_copy(
        src_ref=source,
        dst_ref=target,
        send_sem=send_sem,
        recv_sem=recv_sem,
        device_id=peer,
        device_id_type=pl.DeviceIdType.MESH,
    )


class Places:
    def __init__(self):
        self.tiles = lax.axis_size("tile")
        self.replicas = lax.axis_size("pos")
        self.tile = lax.axis_index("tile")
        self.own = lax.axis_index("pos")
        self.near = flipped(self.own, 1)
        self.far = flipped(self.own, 2)
        self.cross = flipped(self.near, 2)
        self.near_id = {"pos": self.near}
        self.far_id = {"pos": self.far}
        self.up_id = {"tile": lax.rem(self.tile + self.tiles - 1, self.tiles)}
        self.down_id = {"tile": lax.rem(self.tile + 1, self.tiles)}

    def rows(self, first, quarter, count):
        return pl.ds(pl.multiple_of(first + quarter * count, 8), count)


def halo_kernel(
    own_ref, info_ref, measured_ref, ext_ref, info_pair, measured_pair,
    tile_send, tile_recv, far_send, far_recv, near_send, near_recv, pair_send, pair_recv,
):
    at = Places()
    strip = own_ref.shape[1]
    part = strip // at.replicas
    reach = ext_ref.shape[1] // strip - 1
    greet([at.near_id, at.far_id, at.up_id, at.down_id])

    def cols(j):
        piece = own_ref.shape[2] // CUTS
        return pl.ds(j * piece, piece)

    def slot(k, j, quarter):
        return ext_ref.at[:, at.rows(k * strip, quarter, part), cols(j)]

    def up(k, j):
        i = (k - 1) * CUTS + j
        if k == 1:
            source = own_ref.at[:, at.rows(0, at.own, part), cols(j)]
        else:
            source = slot(k - 1, j, at.own)
        return remote(source, slot(k, j, at.own), tile_send.at[i], tile_recv.at[i], at.up_id)

    def across(k, j, quarter):
        i = (k - 1) * CUTS + j
        place = slot(k, j, quarter)
        return remote(place, place, far_send.at[i], far_recv.at[i], at.far_id)

    def beside(k, j, which, quarter):
        i = (k - 1) * CUTS + j
        place = slot(k, j, quarter)
        return remote(place, place, near_send.at[i, which], near_recv.at[i, which], at.near_id)

    def sends(k):
        return jnp.logical_and(at.tile > 0, at.tile + k - 1 < at.tiles)

    @pl.when(sends(1))
    def _():
        for j in range(CUTS):
            up(1, j).start()

    parity = lax.rem(at.own, 2)

    def share(i, place):
        source = (info_ref, measured_ref)[i]
        pair = (info_pair, measured_pair)[i]
        return remote(source, pair.at[place], pair_send.at[i], pair_recv.at[i], at.near_id)

    share(0, parity).start()
    share(1, parity).start()
    info_pair[parity] = info_ref[...]
    measured_pair[parity] = measured_ref[...]
    ext_ref[:, :strip] = own_ref[...]
    for k in range(1, reach + 1):
        @pl.when(at.tile + k >= at.tiles)
        def _(k=k):
            ext_ref[:, k * strip : (k + 1) * strip] = jnp.zeros(own_ref.shape, jnp.float32)

    items = [(k, j) for k in range(1, reach + 1) for j in range(CUTS)]

    def second_hop(k, j):
        @pl.when(at.tile + k < at.tiles)
        def _():
            across(k, j, at.far).wait_recv()
            beside(k, j, 1, at.far).start()

    for i, (k, j) in enumerate(items):
        @pl.when(at.tile + k < at.tiles)
        def _(k=k, j=j):
            up(k, j).wait_recv()

        if k < reach:
            @pl.when(sends(k + 1))
            def _(k=k, j=j):
                up(k + 1, j).start()

        @pl.when(at.tile + k < at.tiles)
        def _(k=k, j=j):
            across(k, j, at.own).start()
            beside(k, j, 0, at.own).start()

        if i > 0:
            second_hop(*items[i - 1])
    second_hop(*items[-1])

    for k, j in items:
        @pl.when(sends(k))
        def _(k=k, j=j):
            up(k, j).wait_send()

        @pl.when(at.tile + k < at.tiles)
        def _(k=k, j=j):
            beside(k, j, 0, at.near).wait_recv()
            beside(k, j, 1, at.cross).wait_recv()
            across(k, j, at.own).wait_send()
            beside(k, j, 0, at.own).wait_send()
            beside(k, j, 1, at.far).wait_send()

    for i in range(2):
        share(i, 1 - parity).wait_recv()
        share(i, parity).wait_send()


def halo(own, info, measured, reach):
    planes, strip, width = own.shape
    vmem = pl.BlockSpec(memory_space=pltpu.VMEM)
    dma = pltpu.SemaphoreType.DMA
    return pl.pallas_call(
        halo_kernel,
        out_shape=(
            jax.ShapeDtypeStruct((planes, strip * (reach + 1), width), jnp.float32),
            jax.ShapeDtypeStruct((2,) + info.shape, jnp.int32),
            jax.ShapeDtypeStruct((2,) + measured.shape, jnp.float32),
        ),
        in_specs=[vmem] * 3,
        out_specs=(vmem,) * 3,
        scratch_shapes=[
            *[dma((reach * CUTS,))] * 4, *[dma((reach * CUTS, 2))] * 2,
            dma((2,)), dma((2,)),
        ],
        compiler_params=pltpu.CompilerParams(
            collective_id=0, has_side_effects=True, vmem_limit_bytes=40 * MIB
        ),
        name="halo",
    )(own, info, measured)


def reduce_kernel(
    stacked_ref, sums_ref, object_ref, probe_ref,
    near_land, far_out, far_land, kept, rim_land, sum_near, sum_far, sum_land, sum_steps, step_land,
    near_send, near_recv, far_send, far_recv, rim_send, rim_recv,
    pn_send, pn_recv, pf_send, pf_recv, step_send, step_recv, out_send, out_recv,
):
    at = Places()
    strip = object_ref.shape[1]
    part = strip // at.replicas
    planes = object_ref.shape[0]
    strips = stacked_ref.shape[1] // strip
    sum_part = sums_ref.shape[1] // at.replicas
    steps = at.tiles.bit_length() - 1
    partners = [{"tile": flipped(at.tile, 2**i)} for i in range(steps)]
    greet([at.near_id, at.far_id, at.up_id, at.down_id] + partners)

    def rows(k, quarter):
        return at.rows(k * strip, quarter, part)

    def sum_rows(quarter):
        return at.rows(0, quarter, sum_part)

    def sum_beside(which, quarter):
        return remote(
            sums_ref.at[:, sum_rows(quarter)], sum_near.at[which], pn_send.at[which], pn_recv.at[which], at.near_id
        )

    width = stacked_ref.shape[2]

    def cols(j):
        return pl.ds(j * (width // CUTS), width // CUTS)

    def beside(k, j, which, quarter):
        return remote(
            stacked_ref.at[:, rows(k, quarter), cols(j)], near_land.at[k, j, which],
            near_send.at[k, j, which], near_recv.at[k, j, which], at.near_id,
        )

    def across(k, j):
        return remote(
            far_out.at[k, j], far_land.at[k, j], far_send.at[k, j], far_recv.at[k, j], at.far_id
        )

    def down(k, j):
        return remote(
            kept.at[k, j], rim_land.at[k - 1, j], rim_send.at[k - 1, j], rim_recv.at[k - 1, j], at.down_id
        )

    def step(i):
        return remote(sum_steps.at[i], step_land.at[i], step_send.at[i], step_recv.at[i], partners[i])

    def object_out(j, lane, quarter, peer):
        place = object_ref.at[:, rows(0, quarter), cols(j)]
        return remote(place, place, out_send.at[1 + j, lane], out_recv.at[1 + j, lane], peer)

    def probe_out(lane, quarter, peer):
        place = probe_ref.at[:, sum_rows(quarter)]
        return remote(place, place, out_send.at[0, lane], out_recv.at[0, lane], peer)

    def probe_update():
        last = sums_ref.shape[0] - 1
        update = -PROBE_RATE * sum_steps[steps, :last] / (sum_steps[steps, last] + RELAX)
        probe_ref[:, sum_rows(at.own)] = update
        probe_out(0, at.own, at.far_id).start()
        probe_out(1, at.own, at.near_id).start()

    sum_across = remote(sum_far, sum_land, pf_send, pf_recv, at.far_id)

    sum_beside(1, at.cross).start()
    sum_beside(0, at.near).start()
    order = [(k, j) for k in range(strips - 1, -1, -1) for j in range(CUTS)]
    for k, j in order:
        beside(k, j, 1, at.cross).start()
    for k, j in order:
        beside(k, j, 0, at.near).start()

    sum_beside(1, at.cross).wait_recv()
    sum_far[...] = sums_ref[:, sum_rows(at.far)] + sum_near[1]
    sum_across.start()
    for k, j in order:
        beside(k, j, 1, at.cross).wait_recv()
        far_out[k, j] = stacked_ref[:, rows(k, at.far), cols(j)] + near_land[k, j, 1]
        across(k, j).start()
    sum_beside(0, at.near).wait_recv()
    total = sums_ref[:, sum_rows(at.own)] + sum_near[0]
    sum_across.wait_recv()
    sum_steps[0] = total + sum_land[...]
    if steps:
        step(0).start()
    for k, j in order:
        beside(k, j, 0, at.near).wait_recv()
        across(k, j).wait_recv()
        kept[k, j] = stacked_ref[:, rows(k, at.own), cols(j)] + near_land[k, j, 0] + far_land[k, j]
        if k < strips - 1:
            @pl.when(at.tile > 0)
            def _(k=k, j=j):
                down(k + 1, j).wait_recv()
                kept[k, j] += rim_land[k, j]

        if k > 0:
            @pl.when(at.tile < at.tiles - 1)
            def _(k=k, j=j):
                down(k, j).start()
        else:
            update = -kept[0, j, :planes] / (kept[0, j, planes] + RELAX)
            object_ref[:, rows(0, at.own), cols(j)] = update
            object_out(j, 0, at.own, at.far_id).start()
            object_out(j, 1, at.own, at.near_id).start()

        i = strips - 1 - k
        if j == CUTS - 1 and i < min(steps, strips - 1):
            step(i).wait_recv()
            sum_steps[i + 1] = sum_steps[i] + step_land[i]
            if i + 1 < steps:
                step(i + 1).start()
            elif i + 1 == steps:
                probe_update()
    for i in range(min(steps, strips - 1), steps):
        step(i).wait_recv()
        sum_steps[i + 1] = sum_steps[i] + step_land[i]
        if i + 1 < steps:
            step(i + 1).start()

    if steps > strips - 1 or steps == 0:
        probe_update()
    outs = [probe_out] + [functools.partial(object_out, j) for j in range(CUTS)]
    for out in outs:
        out(0, at.far, at.far_id).wait_recv()
        out(2, at.far, at.near_id).start()
    for out in outs:
        out(1, at.near, at.near_id).wait_recv()
        out(2, at.cross, at.near_id).wait_recv()
        out(0, at.own, at.far_id).wait_send()
        out(1, at.own, at.near_id).wait_send()
        out(2, at.far, at.near_id).wait_send()

    sum_beside(1, at.cross).wait_send()
    sum_beside(0, at.near).wait_send()
    sum_across.wait_send()
    for k, j in order:
        beside(k, j, 1, at.cross).wait_send()
        beside(k, j, 0, at.near).wait_send()
        across(k, j).wait_send()
        if k > 0:
            @pl.when(at.tile < at.tiles - 1)
            def _(k=k, j=j):
                down(k, j).wait_send()
    for i in range(steps):
        step(i).wait_send()


def reduced(stacked, sums, strip, tiles, replicas):
    planes, ext_rows, width = stacked.shape
    strips = ext_rows // strip
    part = strip // replicas
    sum_planes, side, _ = sums.shape
    sum_part = side // replicas
    steps = tiles.bit_length() - 1
    vmem = pl.BlockSpec(memory_space=pltpu.VMEM)
    dma = pltpu.SemaphoreType.DMA
    block = (planes, part, width // CUTS)
    sum_block = (sum_planes, sum_part, side)

    def buffer(*shape):
        return pltpu.VMEM(shape, jnp.float32)

    return pl.pallas_call(
        reduce_kernel,
        out_shape=(
            jax.ShapeDtypeStruct((planes - 1, strip, width), jnp.float32),
            jax.ShapeDtypeStruct((sum_planes - 1, side, side), jnp.float32),
        ),
        in_specs=[vmem, vmem],
        out_specs=(vmem, vmem),
        scratch_shapes=[
            buffer(strips, CUTS, 2, *block),
            buffer(strips, CUTS, *block),
            buffer(strips, CUTS, *block),
            buffer(strips, CUTS, *block),
            buffer(strips - 1, CUTS, *block),
            buffer(2, *sum_block),
            buffer(*sum_block),
            buffer(*sum_block),
            buffer(steps + 1, *sum_block),
            buffer(max(steps, 1), *sum_block),
            *[dma((strips, CUTS, 2))] * 2, *[dma((strips, CUTS))] * 2, *[dma((strips - 1, CUTS))] * 2,
            dma((2,)), dma((2,)), dma, dma, dma((max(steps, 1),)), dma((max(steps, 1),)), *[dma((1 + CUTS, 3))] * 2,
        ],
        compiler_params=pltpu.CompilerParams(
            collective_id=1, has_side_effects=True, vmem_limit_bytes=48 * MIB
        ),
        name="reduce",
    )(stacked, sums)


def per_device(object_field, probe_modes, measured, row_offset, col_offset, position_count):
    layers, _, strip_rows, width = object_field.shape
    side = probe_modes.shape[2]
    reach = side // strip_rows
    tiles = lax.axis_size("tile")
    replicas = lax.axis_size("pos")
    own = object_field.reshape(2 * layers, strip_rows, width)
    slots_here = row_offset.size
    count = jnp.broadcast_to(position_count.reshape(1, 1), (1, slots_here))
    info = jnp.concatenate(
        [row_offset.reshape(1, -1), col_offset.reshape(1, -1), count], axis=0
    )
    info = jnp.pad(info, ((0, 5), (0, 128 - slots_here)))
    extended, info_pair, measured_pair = halo(own, info, measured.reshape(-1, side, side), reach)
    stacked, sums = slots(info_pair, extended, probe_modes, measured_pair)
    object_flat, probe_flat = reduced(stacked, sums, strip_rows, tiles, replicas)
    return object_flat.reshape(object_field.shape), probe_flat.reshape(probe_modes.shape)


def solution(mesh):
    return jax.shard_map(
        per_device,
        mesh=mesh,
        in_specs=(
            P("groups", None, "tile", None),
            P("groups", None, None, None),
            P(("groups", "tile"), "pos", None, None, None),
            P(("groups", "tile"), "pos", None),
            P(("groups", "tile"), "pos", None),
            P(("groups", "tile"), "pos"),
        ),
        out_specs=(P("groups", None, "tile", None), P("groups", None, None, None)),
        check_vma=False,
    )
```
